128 devices in a mesh: ctx: 16 (over z_hi, x, core), kv: 8 (over y, z_lo).
Axes of the slice: x: 4, y: 4, z: 4 (z_hi: 2, z_lo: 2; z = z_hi * 2 + z_lo), core: 2. Of those that a mesh axis runs over, the one named last changes fastest.
Arguments:
- queries: bfloat16 [8192, 64, 128], P('ctx', 'kv'), may hold values from -5 to 5
- key_heads: bfloat16 [8192, 8, 128], P('ctx', 'kv'), may hold values from -5 to 5
- value_head_rows: bfloat16 [8192, 8, 128], P('ctx', 'kv'), may hold values from -6 to 6
- out_grad: bfloat16 [8192, 64, 128], P('ctx', 'kv'), may hold values from -96 to 96
- doc_start: int32 [8192], P(('ctx', 'kv')), may hold values from 0 to 8191, as said below
Outputs:
- query_grad: bfloat16 [8192, 64, 128], P('ctx', 'kv')
- key_grad: bfloat16 [8192, 8, 128], P('ctx', 'kv')
- value_grad: bfloat16 [8192, 8, 128], P('ctx', 'kv')
The draws below stay inside these ranges and needn't reach their ends.
Inputs may be any that keep to these rules, and one draw needn't show every extreme that they name: doc_start[p] is the first position of the document holding p: doc_start[p] <= p, and doc_start[p] equals p or doc_start[p - 1]; the last position starts a document of its own.
All inputs are finite; a program needn't handle non-finite values.
Results may differ from the reference program's by a relative error of at most 0.04.
Values may be sent and summed in bfloat16 or wider, within the bound.
No kernel may reach another device: no remote copies, remote signals or barrier semaphores. Data moves between devices by JAX's collectives and lax.ppermute only.
A program may use at most 192 MiB of HBM per device.

```python
import math
import jax
import jax.numpy as jnp
from jax import lax

HEAD_SIZE = 128
KEY_VALUE_HEADS = 8
HQ = 64
SPAN = 4
TOK_DEV = 512
PACKED_TOKENS = 8192


def draw_queries(key, part):
    key = jax.random.fold_in(key, 1)
    window_start = jnp.clip(jax.random.normal(key, (PACKED_TOKENS, HQ, HEAD_SIZE), jnp.float32), -4.5, 4.5)
    return window_start.astype(jnp.bfloat16)


def draw_key_heads(key, part):
    key = jax.random.fold_in(key, 2)
    window_start = jnp.clip(jax.random.normal(key, (PACKED_TOKENS, KEY_VALUE_HEADS, HEAD_SIZE), jnp.float32), -4.5, 4.5)
    return window_start.astype(jnp.bfloat16)


def draw_doc_start(key, part):
    key = jax.random.fold_in(key, 3)
    lengths = jax.random.randint(key, (PACKED_TOKENS,), TOK_DEV // 4, 2 * SPAN * TOK_DEV)
    ends = jnp.minimum(jnp.cumsum(lengths), PACKED_TOKENS)
    marks = jnp.zeros((PACKED_TOKENS + 1,), jnp.int32).at[ends].set(1)[:PACKED_TOKENS].at[0].set(1).at[PACKED_TOKENS - 1].set(1)
    places = jnp.arange(PACKED_TOKENS, dtype=jnp.int32)
    return lax.cummax(places * marks, axis=0)


def block_levels(key, shape, cuts, smallest, high):
    gain, own = 1.0, jax.random.fold_in(key, 6)
    for position, shards_of in cuts:
        draws = jnp.exp(jax.random.uniform(jax.random.fold_in(own, position), (shards_of,), jnp.float32, smallest / len(cuts), high / len(cuts)))
        gain = gain * jnp.repeat(draws, shape[position] // shards_of).reshape([-1 if axis == position else 1 for axis in range(len(shape))])
    return gain


def bell_draw(key, dims, width, bound, split=(), kind=jnp.bfloat16):
    level = block_levels(key, dims, split, -0.22, 0.18) if split else 1.0
    entries = jax.random.normal(key, dims, jnp.float32) * width * level
    return jnp.minimum(jnp.maximum(entries, -bound), bound).astype(kind)


def setup_inputs(seed: int = 0) -> dict:
    splits = jax.random.split(jax.random.key(seed), 6)
    return {
        "queries": draw_queries(jax.random.fold_in(splits[5], 71), 0),
        "key_heads": draw_key_heads(jax.random.fold_in(splits[5], 71), 0),
        "value_head_rows": bell_draw(splits[2], (PACKED_TOKENS, KEY_VALUE_HEADS, HEAD_SIZE), 1.0, 6.0, ((0, 16), (1, 8))),
        "out_grad": bell_draw(splits[3], (PACKED_TOKENS, HQ, HEAD_SIZE), 16.0, 96.0, ((0, 16), (1, 8))),
        "doc_start": draw_doc_start(jax.random.fold_in(splits[5], 71), 0),
    }


fill_value = -1e+30

def round_keep(values):
    return lax.optimization_barrier(values.astype(jnp.bfloat16)).astype(jnp.float32)

def reference(queries, key_heads, value_head_rows, out_grad, doc_start):
    token_count, head_count, head_width = queries.shape
    group_count = key_heads.shape[1]
    per_group = head_count // group_count
    block_len = TOK_DEV
    window = SPAN * block_len
    lead_rows = (SPAN - 1) * block_len
    logit_scale = 1.0 / math.sqrt(head_width)
    lead = jnp.zeros((lead_rows, group_count, head_width), key_heads.dtype)
    keys_padded = jnp.concatenate([lead, key_heads], 0)
    values_padded = jnp.concatenate([lead, value_head_rows], 0)

    def visit_block(carried, block_index):
        key_acc, value_acc = carried
        start = (block_index * block_len).astype(jnp.int32)
        query_block = lax.dynamic_slice_in_dim(queries, start, block_len, 0).reshape(block_len, group_count, per_group, head_width).astype(jnp.float32)
        gradient_block = lax.dynamic_slice_in_dim(out_grad, start, block_len, 0).reshape(block_len, group_count, per_group, head_width).astype(jnp.float32)
        bounds = lax.dynamic_slice_in_dim(doc_start, start, block_len, 0)
        key_window = lax.dynamic_slice_in_dim(keys_padded, start, window, 0).astype(jnp.float32)
        value_window = lax.dynamic_slice_in_dim(values_padded, start, window, 0).astype(jnp.float32)
        query_pos = start + jnp.arange(block_len, dtype=jnp.int32)
        key_pos = start - lead_rows + jnp.arange(window, dtype=jnp.int32)
        allowed = (key_pos[None, :] <= query_pos[:, None]) & (key_pos[None, :] >= bounds[:, None])
        raw_scores = jnp.einsum('mpeb,hpb->pemh', query_block, key_window) * logit_scale
        scores = jnp.where(allowed[None, None], raw_scores, fill_value)
        row_max = lax.optimization_barrier(jnp.max(scores, -1))
        unscaled = jnp.where(allowed[None, None], jnp.exp(scores - row_max[..., None]), 0.0)
        totals = lax.optimization_barrier(jnp.sum(unscaled, -1))
        softmax_weights = round_keep(unscaled)
        summed_rows = jnp.einsum('fjqw,wfk->qfjk', softmax_weights, value_window)
        attn_out = (summed_rows / jnp.transpose(totals, (2, 0, 1))[..., None]).astype(jnp.bfloat16)
        row_dot = lax.optimization_barrier(jnp.sum(gradient_block * attn_out.astype(jnp.float32), -1))
        attn_prob = unscaled / totals[..., None]
        probability_block = round_keep(attn_prob)
        value_portion = jnp.einsum('qnjo,jqnu->oqu', probability_block, gradient_block)
        probability_gradient = jnp.einsum('mpeb,hpb->pemh', gradient_block, value_window)
        score_gradient = round_keep(attn_prob * (probability_gradient - jnp.transpose(row_dot, (1, 2, 0))[..., None]) * logit_scale)
        query_portion = jnp.einsum('fjqw,wfk->qfjk', score_gradient, key_window)
        key_portion = jnp.einsum('qnjo,jqnu->oqu', score_gradient, query_block)
        key_acc = lax.dynamic_update_slice_in_dim(key_acc, lax.dynamic_slice_in_dim(key_acc, start, window, 0) + key_portion, start, 0)
        value_acc = lax.dynamic_update_slice_in_dim(value_acc, lax.dynamic_slice_in_dim(value_acc, start, window, 0) + value_portion, start, 0)
        return ((key_acc, value_acc), query_portion.astype(jnp.bfloat16).reshape(block_len, head_count, head_width))
    empty = jnp.zeros((lead_rows + token_count, group_count, head_width), jnp.float32)
    (key_acc, value_acc), query_blocks = lax.scan(visit_block, (empty, empty), jnp.arange(token_count // block_len, dtype=jnp.int32))
    query_grad = query_blocks.reshape(token_count, head_count, head_width)
    key_grad = key_acc[lead_rows:].astype(jnp.bfloat16)
    value_grad = value_acc[lead_rows:].astype(jnp.bfloat16)
    return (query_grad, key_grad, value_grad)
```

```python
import functools
import math

import jax
import jax.numpy as jnp
from jax import lax
from jax.experimental import pallas as pl
from jax.experimental.pallas import tpu as pltpu
from jax.sharding import PartitionSpec as P

SPAN = 4
BLOCK = 512
HEADS = 8
WIDTH = 128
TILES = 8
ROWS = BLOCK * HEADS // TILES
TOKENS = BLOCK // TILES
SCALE = 1.0 / math.sqrt(WIDTH)
EXP2_SCALE = SCALE * math.log2(math.e)
FILL = -1e30

VMEM = pl.BlockSpec(memory_space=pltpu.VMEM)
SMEM = pl.BlockSpec(memory_space=pltpu.SMEM)
F32 = jnp.float32
BF16 = jnp.bfloat16


def dot(a, b, ca, cb):
    return lax.dot_general(a, b, (((ca,), (cb,)), ((), ())), preferred_element_type=F32)


def tile_rows(t):
    if isinstance(t, int):
        return pl.ds(t * ROWS, ROWS)
    return pl.ds(pl.multiple_of(t * ROWS, ROWS), ROWS)


def own_extent(t):
    return 128 * ((t * TOKENS + TOKENS - 1) // 128 + 1)


def masked_scores(scores, bounds, offset, t):
    key = lax.broadcasted_iota(jnp.int32, scores.shape, 0) - offset * BLOCK
    if offset:
        return jnp.where(key >= bounds, scores, FILL)
    token = t * TOKENS + lax.broadcasted_iota(jnp.int32, (1, scores.shape[1]), 1) // HEADS
    return jnp.where((key >= bounds) & (key <= token), scores, FILL)


def reached_tiles(first_ref, offset):
    count = jnp.int32(0)
    for t in range(TILES):
        count += (first_ref[t, 0] < (1 - offset) * BLOCK).astype(jnp.int32)
    return count


def over_tiles(first_ref, offset, visit):
    if offset == 0:
        for t in range(TILES):
            visit(t)
        return
    count = reached_tiles(first_ref, offset)

    @pl.when(count == TILES)
    def _():
        for t in range(TILES):
            visit(t)

    @pl.when(count < TILES)
    def _():
        lax.fori_loop(0, count, lambda t, c: (visit(t), c)[1], 0)


def stats_kernel(offsets, *refs):
    count = len(offsets)
    first_ref, bound_ref, q_ref, g_ref = refs[:4]
    kv_refs = refs[4 : 4 + 2 * count]
    rest = refs[4 + 2 * count :]
    if offsets[0] == 0:
        m_ref, l_ref, d_ref = rest
    else:
        m_in, l_in, d_in, m_ref, l_ref, d_ref = rest
        m_ref[...] = m_in[...]
        l_ref[...] = l_in[...]
        d_ref[...] = d_in[...]

    for place, offset in enumerate(offsets):
        k_ref, v_ref = kv_refs[2 * place : 2 * place + 2]

        def visit(t, offset=offset, k_ref=k_ref, v_ref=v_ref):
            rows = tile_rows(t)
            one = pl.ds(t, 1)
            extent = own_extent(t) if offset == 0 else BLOCK
            scores = dot(k_ref[0:extent, :], q_ref[rows, :], 1, 1)
            scores = masked_scores(scores, bound_ref[one, :], offset, t)
            prob_grad = dot(v_ref[0:extent, :], g_ref[rows, :], 1, 1)
            top = jnp.max(scores, 0, keepdims=True)
            if offset:
                before = m_ref[one, :]
                top = jnp.maximum(top, before)
            unscaled = jnp.exp2(scores * EXP2_SCALE - top * EXP2_SCALE)
            total = jnp.sum(unscaled, 0, keepdims=True)
            product = jnp.sum(unscaled * prob_grad, 0, keepdims=True)
            if offset:
                decay = jnp.exp2((before - top) * EXP2_SCALE)
                total += l_ref[one, :] * decay
                product += d_ref[one, :] * decay
            m_ref[one, :] = top
            l_ref[one, :] = total
            d_ref[one, :] = product

        over_tiles(first_ref, offset, visit)

    if offsets[-1] == SPAN - 1:
        total = l_ref[...]
        m_ref[...] = m_ref[...] * EXP2_SCALE + jnp.log2(total)
        d_ref[...] = d_ref[...] / total


def stats(offsets, first, bounds, q, g, kv, carried):
    shape = jax.ShapeDtypeStruct((TILES, ROWS), F32)
    operands = [first, bounds, q, g]
    for offset in offsets:
        operands += list(kv[offset])
    operands += list(carried)
    work = sum(BLOCK if o else BLOCK * 5 // 8 for o in offsets) * TILES * ROWS
    return pl.pallas_call(
        functools.partial(stats_kernel, offsets),
        in_specs=[SMEM] + [VMEM] * (len(operands) - 1),
        out_specs=[VMEM] * 3,
        out_shape=[shape] * 3,
        compiler_params=pltpu.CompilerParams(vmem_limit_bytes=40 << 20),
        cost_estimate=pl.CostEstimate(
            flops=4 * WIDTH * work, bytes_accessed=3 << 20, transcendentals=work
        ),
        name="stats_" + "_".join(str(o) for o in offsets),
    )(*operands)


def grad_kernel(offset, *refs):
    first_ref, bound_ref, q_ref, g_ref, k_ref, v_ref, m_ref, d_ref = refs[:8]
    if offset == SPAN - 1:
        dq_ref, pair_ref, key_acc, value_acc = refs[8:]
        dq_in = None
    elif offset:
        dq_in, dq_ref, pair_ref, key_acc, value_acc = refs[8:]
    else:
        dq_in, dq_ref, pair_ref, key_acc, value_acc = refs[8:]
    key_acc[...] = jnp.zeros_like(key_acc)
    value_acc[...] = jnp.zeros_like(value_acc)
    if offset == SPAN - 1:
        dq_ref[...] = jnp.zeros_like(dq_ref)

    def visit(t):
        rows = tile_rows(t)
        one = pl.ds(t, 1)
        extent = own_extent(t) if offset == 0 else BLOCK
        keys = k_ref[0:extent, :]
        scores = dot(keys, q_ref[rows, :], 1, 1)
        scores = masked_scores(scores, bound_ref[one, :], offset, t)
        prob_grad = dot(v_ref[0:extent, :], g_ref[rows, :], 1, 1)
        prob = jnp.exp2(scores * EXP2_SCALE - m_ref[one, :])
        score_grad = (prob * (prob_grad - d_ref[one, :])).astype(BF16)
        value_acc[0:extent, :] += dot(prob.astype(BF16), g_ref[rows, :], 1, 0)
        key_acc[0:extent, :] += dot(score_grad, q_ref[rows, :], 1, 0)
        part = dot(keys, score_grad, 0, 0)
        if offset == 0:
            dq_ref[rows, :] = jnp.transpose((dq_in[:, rows] + part) * SCALE).astype(BF16)
        else:
            dq_ref[:, rows] += part

    over_tiles(first_ref, offset, visit)
    pair_ref[0] = (key_acc[...] * SCALE).astype(pair_ref.dtype)
    pair_ref[1] = value_acc[...].astype(pair_ref.dtype)


def grad(offset, first, bounds, q, g, pair, lse, row_dot, dq):
    operands = [first, bounds, q, g, pair[0], pair[1], lse, row_dot]
    aliases = {}
    if offset < SPAN - 1:
        operands.append(dq)
        if offset:
            aliases = {len(operands) - 1: 0}
    if offset:
        dq_shape = jax.ShapeDtypeStruct((WIDTH, TILES * ROWS), F32)
    else:
        dq_shape = jax.ShapeDtypeStruct((TILES * ROWS, WIDTH), BF16)
    work = (BLOCK if offset else BLOCK * 5 // 8) * TILES * ROWS
    return pl.pallas_call(
        functools.partial(grad_kernel, offset),
        in_specs=[SMEM] + [VMEM] * (len(operands) - 1),
        out_specs=[VMEM] * 2,
        out_shape=[dq_shape, jax.ShapeDtypeStruct((2, BLOCK, WIDTH), BF16 if offset else F32)],
        scratch_shapes=[pltpu.VMEM((BLOCK, WIDTH), F32)] * 2,
        input_output_aliases=aliases,
        compiler_params=pltpu.CompilerParams(vmem_limit_bytes=40 << 20),
        cost_estimate=pl.CostEstimate(
            flops=10 * WIDTH * work, bytes_accessed=7 << 20, transcendentals=work
        ),
        name="grad_%d" % offset,
    )(*operands)


def shift(value, steps):
    count = lax.axis_size("ctx")
    first, last = (max(0, -steps), min(count, count - steps))
    return lax.ppermute(value, "ctx", [(s, s + steps) for s in range(first, last)])


def local(queries, key_heads, value_head_rows, out_grad, doc_start):
    block_len, head_count, head_width = queries.shape
    ctx = lax.axis_index("ctx")
    member = lax.axis_index("kv")
    members = lax.axis_size("kv")
    q = queries.reshape(block_len * head_count, head_width)
    g = out_grad.reshape(block_len * head_count, head_width)
    k = key_heads.reshape(block_len, head_width)
    v = value_head_rows.reshape(block_len, head_width)

    own = jnp.repeat(doc_start - ctx * block_len, head_count)[None, :]
    place = lax.broadcasted_iota(jnp.int32, (members, 1), 0)
    bounds = jnp.where(place == member, own, 0)
    step = 1
    while step < members:
        bounds = bounds + lax.ppermute(bounds, "kv", [(s, s ^ step) for s in range(members)])
        step *= 2
    first = bounds[:, :1]

    both = jnp.stack([k, v])
    one = shift(both, 1)
    two = shift(both, 2)
    three = shift(two, 1)
    kv = [(k, v)] + [(a[0], a[1]) for a in (one, two, three)]

    carried = stats((0, 1), first, bounds, q, g, kv, ())
    lse, _, row_dot = stats((2, 3), first, bounds, q, g, kv, carried)
    dq, pair3 = grad(3, first, bounds, q, g, kv[3], lse, row_dot, None)
    back3 = shift(pair3, -3)
    dq, pair2 = grad(2, first, bounds, q, g, kv[2], lse, row_dot, dq)
    back2 = shift(pair2, -2)
    dq, pair1 = grad(1, first, bounds, q, g, kv[1], lse, row_dot, dq)
    back1 = shift(pair1, -1)
    dq, pair0 = grad(0, first, bounds, q, g, kv[0], lse, row_dot, dq)
    total = pair0 + back3.astype(F32) + back2.astype(F32) + back1.astype(F32)
    total = total.astype(BF16)
    return (
        dq.reshape(queries.shape),
        total[0].reshape(key_heads.shape),
        total[1].reshape(value_head_rows.shape),
    )


def solution(mesh):
    return jax.shard_map(
        local,
        mesh=mesh,
        in_specs=(
            P("ctx", "kv", None),
            P("ctx", "kv", None),
            P("ctx", "kv", None),
            P("ctx", "kv", None),
            P(("ctx", "kv")),
        ),
        out_specs=(P("ctx", "kv", None), P("ctx", "kv", None), P("ctx", "kv", None)),
        check_vma=False,
    )
```

```python
import functools
import math

import jax
import jax.numpy as jnp
from jax import lax
from jax.experimental import pallas as pl
from jax.experimental.pallas import tpu as pltpu
from jax.sharding import PartitionSpec as P

SPAN = 4
BLOCK = 512
HEADS = 8
WIDTH = 128
TILES = 8
ROWS = BLOCK * HEADS // TILES
TOKENS = BLOCK // TILES
SCALE = 1.0 / math.sqrt(WIDTH)
EXP2_SCALE = SCALE * math.log2(math.e)
FILL = -1e30

VMEM = pl.BlockSpec(memory_space=pltpu.VMEM)
SMEM = pl.BlockSpec(memory_space=pltpu.SMEM)
F32 = jnp.float32
BF16 = jnp.bfloat16


def dot(a, b, ca, cb):
    return lax.dot_general(a, b, (((ca,), (cb,)), ((), ())), preferred_element_type=F32)


def tile_rows(t):
    if isinstance(t, int):
        return pl.ds(t * ROWS, ROWS)
    return pl.ds(pl.multiple_of(t * ROWS, ROWS), ROWS)


def own_extent(t):
    return 128 * ((t * TOKENS + TOKENS - 1) // 128 + 1)


def masked_scores(scores, bounds, offset, t):
    key = lax.broadcasted_iota(jnp.int32, scores.shape, 0) - offset * BLOCK
    if offset:
        return jnp.where(key >= bounds, scores, FILL)
    token = t * TOKENS + lax.broadcasted_iota(jnp.int32, (1, scores.shape[1]), 1) // HEADS
    return jnp.where((key >= bounds) & (key <= token), scores, FILL)


def reached_tiles(first_ref, offset):
    count = jnp.int32(0)
    for t in range(TILES):
        count += (first_ref[t, 0] < (1 - offset) * BLOCK).astype(jnp.int32)
    return count


def over_tiles(first_ref, offset, visit):
    if offset == 0:
        for t in range(TILES):
            visit(t)
        return
    count = reached_tiles(first_ref, offset)

    @pl.when(count == TILES)
    def _():
        for t in range(TILES):
            visit(t)

    @pl.when(count < TILES)
    def _():
        lax.fori_loop(0, count, lambda t, c: (visit(t), c)[1], 0)


def stats_kernel(offsets, *refs):
    count = len(offsets)
    first_ref, bound_ref, q_ref, g_ref = refs[:4]
    kv_refs = refs[4 : 4 + 2 * count]
    rest = refs[4 + 2 * count :]
    if offsets[0] == 0:
        m_ref, l_ref, d_ref = rest
    else:
        m_in, l_in, d_in, m_ref, l_ref, d_ref = rest
        m_ref[...] = m_in[...]
        l_ref[...] = l_in[...]
        d_ref[...] = d_in[...]

    for place, offset in enumerate(offsets):
        k_ref, v_ref = kv_refs[2 * place : 2 * place + 2]

        def visit(t, offset=offset, k_ref=k_ref, v_ref=v_ref):
            rows = tile_rows(t)
            one = pl.ds(t, 1)
            extent = own_extent(t) if offset == 0 else BLOCK
            scores = dot(k_ref[0:extent, :], q_ref[rows, :], 1, 1)
            scores = masked_scores(scores, bound_ref[one, :], offset, t)
            prob_grad = dot(v_ref[0:extent, :], g_ref[rows, :], 1, 1)
            top = jnp.max(scores, 0, keepdims=True)
            if offset:
                before = m_ref[one, :]
                top = jnp.maximum(top, before)
            unscaled = jnp.exp2(scores * EXP2_SCALE - top * EXP2_SCALE)
            total = jnp.sum(unscaled, 0, keepdims=True)
            product = jnp.sum(unscaled * prob_grad, 0, keepdims=True)
            if offset:
                decay = jnp.exp2((before - top) * EXP2_SCALE)
                total += l_ref[one, :] * decay
                product += d_ref[one, :] * decay
            m_ref[one, :] = top
            l_ref[one, :] = total
            d_ref[one, :] = product

        over_tiles(first_ref, offset, visit)


def stats(offsets, first, bounds, q, g, kv, carried):
    shape = jax.ShapeDtypeStruct((TILES, ROWS), F32)
    operands = [first, bounds, q, g]
    for offset in offsets:
        operands += list(kv[offset])
    operands += list(carried)
    work = sum(BLOCK if o else BLOCK * 5 // 8 for o in offsets) * TILES * ROWS
    return pl.pallas_call(
        functools.partial(stats_kernel, offsets),
        in_specs=[SMEM] + [VMEM] * (len(operands) - 1),
        out_specs=[VMEM] * 3,
        out_shape=[shape] * 3,
        compiler_params=pltpu.CompilerParams(vmem_limit_bytes=40 << 20),
        cost_estimate=pl.CostEstimate(
            flops=work, bytes_accessed=1 << 10, transcendentals=0
        ),
        name="stats_" + "_".join(str(o) for o in offsets),
    )(*operands)


def far_kernel(
    first_ref, bound_ref, q_ref, g_ref, k_ref, v_ref, m_ref, l_ref, d_in,
    lse_ref, d_ref, dq_ref, pair_ref, key_acc, value_acc,
):
    offset = SPAN - 1
    key_acc[...] = jnp.zeros_like(key_acc)
    value_acc[...] = jnp.zeros_like(value_acc)
    dq_ref[...] = jnp.zeros_like(dq_ref)
    lse_ref[...] = m_ref[...] * EXP2_SCALE + jnp.log2(l_ref[...])
    d_ref[...] = d_in[...] / l_ref[...]

    def visit(t):
        rows = tile_rows(t)
        one = pl.ds(t, 1)
        scores = dot(k_ref[...], q_ref[rows, :], 1, 1)
        scores = masked_scores(scores, bound_ref[one, :], offset, t)
        prob_grad = dot(v_ref[...], g_ref[rows, :], 1, 1)
        before = m_ref[one, :]
        top = jnp.maximum(jnp.max(scores, 0, keepdims=True), before)
        unscaled = jnp.exp2(scores * EXP2_SCALE - top * EXP2_SCALE)
        decay = jnp.exp2((before - top) * EXP2_SCALE)
        total = jnp.sum(unscaled, 0, keepdims=True) + l_ref[one, :] * decay
        product = jnp.sum(unscaled * prob_grad, 0, keepdims=True) + d_in[one, :] * decay
        inverse = 1.0 / total
        row_dot = product * inverse
        lse_ref[one, :] = top * EXP2_SCALE + jnp.log2(total)
        d_ref[one, :] = row_dot
        prob = unscaled * inverse
        score_grad = (prob * (prob_grad - row_dot)).astype(BF16)
        value_acc[...] += dot(prob.astype(BF16), g_ref[rows, :], 1, 0)
        key_acc[...] += dot(score_grad, q_ref[rows, :], 1, 0)
        dq_ref[:, rows] = dot(k_ref[...], score_grad, 0, 0)

    over_tiles(first_ref, offset, visit)
    pair_ref[0] = (key_acc[...] * SCALE).astype(pair_ref.dtype)
    pair_ref[1] = value_acc[...].astype(pair_ref.dtype)


def far_grad(first, bounds, q, g, pair, carried):
    row = jax.ShapeDtypeStruct((TILES, ROWS), F32)
    return pl.pallas_call(
        far_kernel,
        in_specs=[SMEM] + [VMEM] * 8,
        out_specs=[VMEM] * 4,
        out_shape=[
            row,
            row,
            jax.ShapeDtypeStruct((WIDTH, TILES * ROWS), F32),
            jax.ShapeDtypeStruct((2, BLOCK, WIDTH), BF16),
        ],
        scratch_shapes=[pltpu.VMEM((BLOCK, WIDTH), F32)] * 2,
        compiler_params=pltpu.CompilerParams(vmem_limit_bytes=40 << 20),
        cost_estimate=pl.CostEstimate(flops=1 << 20, bytes_accessed=1 << 10, transcendentals=0),
        name="grad_far",
    )(first, bounds, q, g, pair[0], pair[1], *carried)


def grad_kernel(offset, *refs):
    first_ref, bound_ref, q_ref, g_ref, k_ref, v_ref, m_ref, d_ref = refs[:8]
    dq_in, dq_ref, dk_ref, dv_ref, key_acc, value_acc = refs[8:]
    key_acc[...] = jnp.zeros_like(key_acc)
    value_acc[...] = jnp.zeros_like(value_acc)

    def visit(t):
        rows = tile_rows(t)
        one = pl.ds(t, 1)
        extent = own_extent(t) if offset == 0 else BLOCK
        keys = k_ref[0:extent, :]
        scores = dot(keys, q_ref[rows, :], 1, 1)
        scores = masked_scores(scores, bound_ref[one, :], offset, t)
        prob_grad = dot(v_ref[0:extent, :], g_ref[rows, :], 1, 1)
        prob = jnp.exp2(scores * EXP2_SCALE - m_ref[one, :])
        score_grad = (prob * (prob_grad - d_ref[one, :])).astype(BF16)
        value_acc[0:extent, :] += dot(prob.astype(BF16), g_ref[rows, :], 1, 0)
        key_acc[0:extent, :] += dot(score_grad, q_ref[rows, :], 1, 0)
        part = dot(keys, score_grad, 0, 0)
        if offset == 0:
            dq_ref[rows, :] = jnp.transpose(((dq_in[:, rows] + part) * SCALE).astype(BF16))
        else:
            dq_ref[:, rows] += part

    over_tiles(first_ref, offset, visit)
    dk_ref[...] = key_acc[...] * SCALE
    dv_ref[...] = value_acc[...]


def grad(offset, first, bounds, q, g, pair, lse, row_dot, dq):
    operands = [first, bounds, q, g, pair[0], pair[1], lse, row_dot, dq]
    if offset:
        dq_shape = jax.ShapeDtypeStruct((WIDTH, TILES * ROWS), F32)
    else:
        dq_shape = jax.ShapeDtypeStruct((TILES * ROWS, WIDTH), BF16)
    return pl.pallas_call(
        functools.partial(grad_kernel, offset),
        in_specs=[SMEM] + [VMEM] * (len(operands) - 1),
        out_specs=[VMEM] * 3,
        out_shape=[dq_shape] + [jax.ShapeDtypeStruct((BLOCK, WIDTH), F32)] * 2,
        scratch_shapes=[pltpu.VMEM((BLOCK, WIDTH), F32)] * 2,
        input_output_aliases={8: 0} if offset else {},
        compiler_params=pltpu.CompilerParams(vmem_limit_bytes=40 << 20),
        cost_estimate=pl.CostEstimate(flops=1 << 20, bytes_accessed=1 << 10, transcendentals=0),
        name="grad_%d" % offset,
    )(*operands)


def ring(value, steps):
    count = lax.axis_size("ctx")
    return lax.ppermute(value, "ctx", [(s, (s + steps) % count) for s in range(count)])


def pair_swap(value):
    return lax.ppermute(value, "ctx", [(s, s ^ 1) for s in range(lax.axis_size("ctx"))])


def near_and_far(value):
    count = lax.axis_size("ctx")
    return lax.ppermute(
        value, "ctx", [(s, s + 1 if s % 2 == 0 else (s + 3) % count) for s in range(count)]
    )


def local(queries, key_heads, value_head_rows, out_grad, doc_start):
    block_len, head_count, head_width = queries.shape
    ctx = lax.axis_index("ctx")
    member = lax.axis_index("kv")
    members = lax.axis_size("kv")
    q = queries.reshape(block_len * head_count, head_width)
    g = out_grad.reshape(block_len * head_count, head_width)
    k = key_heads.reshape(block_len, head_width)
    v = value_head_rows.reshape(block_len, head_width)

    own = jnp.repeat(doc_start - ctx * block_len, head_count)[None, :]
    place = lax.broadcasted_iota(jnp.int32, (members, 1), 0)
    bounds = jnp.where(place == member, own, 0)
    step = 1
    while step < members:
        bounds = bounds + lax.ppermute(bounds, "kv", [(s, s ^ step) for s in range(members)])
        step *= 2
    first = bounds[:, :1]

    both = jnp.stack([k, v])
    two = ring(both, 2)
    mixed = near_and_far(both)
    swapped = pair_swap(two)
    even = ctx % 2 == 0
    one = jnp.where(even, swapped, mixed)
    three = jnp.where(even, mixed, swapped)
    kv = [(k, v)] + [(a[0], a[1]) for a in (one, two, three)]

    carried = stats((0, 2), first, bounds, q, g, kv, ())
    carried = stats((1,), first, bounds, q, g, kv, carried)
    lse, row_dot, dq, chain = far_grad(first, bounds, q, g, kv[3], carried)
    for offset in (2, 1):
        back = ring(chain, -1)
        dq, dk, dv = grad(offset, first, bounds, q, g, kv[offset], lse, row_dot, dq)
        chain = (jnp.stack([dk, dv]) + back.astype(F32)).astype(BF16)
    back = ring(chain, -1).astype(F32)
    dq, dk, dv = grad(0, first, bounds, q, g, kv[0], lse, row_dot, dq)
    return (
        dq.reshape(queries.shape),
        (dk + back[0]).astype(BF16).reshape(key_heads.shape),
        (dv + back[1]).astype(BF16).reshape(value_head_rows.shape),
    )


def solution(mesh):
    return jax.shard_map(
        local,
        mesh=mesh,
        in_specs=(
            P("ctx", "kv", None),
            P("ctx", "kv", None),
            P("ctx", "kv", None),
            P("ctx", "kv", None),
            P(("ctx", "kv")),
        ),
        out_specs=(P("ctx", "kv", None), P("ctx", "kv", None), P("ctx", "kv", None)),
        check_vma=False,
    )
```

```python
import functools
import math

import jax
import jax.numpy as jnp
from jax import lax
from jax.experimental import pallas as pl
from jax.experimental.pallas import tpu as pltpu
from jax.sharding import PartitionSpec as P

SPAN = 4
BLOCK = 512
HEADS = 8
WIDTH = 128
TILES = 8
ROWS = BLOCK * HEADS // TILES
TOKENS = BLOCK // TILES
SCALE = 1.0 / math.sqrt(WIDTH)
EXP2_SCALE = SCALE * math.log2(math.e)
FILL = -1e30
PIECE = 256
PIECES = BLOCK // PIECE
NEAR = SPAN - 1

VMEM = pl.BlockSpec(memory_space=pltpu.VMEM)
SMEM = pl.BlockSpec(memory_space=pltpu.SMEM)
F32 = jnp.float32
BF16 = jnp.bfloat16


def dot(a, b, ca, cb):
    return lax.dot_general(a, b, (((ca,), (cb,)), ((), ())), preferred_element_type=F32)


def tile_rows(t):
    if isinstance(t, int):
        return pl.ds(t * ROWS, ROWS)
    return pl.ds(pl.multiple_of(t * ROWS, ROWS), ROWS)


def own_extent(t):
    return 128 * ((t * TOKENS + TOKENS - 1) // 128 + 1)


def masked_scores(scores, bounds, offset, t):
    key = lax.broadcasted_iota(jnp.int32, scores.shape, 0) - offset * BLOCK
    if offset:
        return jnp.where(key >= bounds, scores, FILL)
    token = t * TOKENS + lax.broadcasted_iota(jnp.int32, (1, scores.shape[1]), 1) // HEADS
    return jnp.where((key >= bounds) & (key <= token), scores, FILL)


def reached_tiles(first_ref, offset):
    count = jnp.int32(0)
    for t in range(TILES):
        count += (first_ref[t, 0] < (1 - offset) * BLOCK).astype(jnp.int32)
    return count


def over_tiles(first_ref, offset, visit):
    if offset == 0:
        for t in range(TILES):
            visit(t)
        return
    count = reached_tiles(first_ref, offset)

    @pl.when(count == TILES)
    def _():
        for t in range(TILES):
            visit(t)

    @pl.when(count < TILES)
    def _():
        lax.fori_loop(0, count, lambda t, c: (visit(t), c)[1], 0)


def piece_kernel(offset, q_ref, g_ref, k_ref, v_ref, m_ref, l_ref, d_ref):
    if offset == 0:
        m_ref[...] = jnp.full_like(m_ref, FILL)
        l_ref[...] = jnp.zeros_like(l_ref)
        d_ref[...] = jnp.zeros_like(d_ref)
    for t in range(TILES):
        rows = tile_rows(t)
        for c in range(PIECES):
            begin = c * PIECE
            end = begin + PIECE
            if offset == 0:
                end = min(end, own_extent(t))
                if end <= begin:
                    continue
            scores = dot(k_ref[begin:end, :], q_ref[rows, :], 1, 1)
            if offset == 0 and end > t * TOKENS:
                key = begin + lax.broadcasted_iota(jnp.int32, scores.shape, 0)
                token = t * TOKENS + lax.broadcasted_iota(jnp.int32, (1, ROWS), 1) // HEADS
                scores = jnp.where(key <= token, scores, FILL)
            prob_grad = dot(v_ref[begin:end, :], g_ref[rows, :], 1, 1)
            top = jnp.max(scores, 0, keepdims=True)
            unscaled = jnp.exp2(scores * EXP2_SCALE - top * EXP2_SCALE)
            m_ref[c, t : t + 1, :] = top
            l_ref[c, t : t + 1, :] = jnp.sum(unscaled, 0, keepdims=True)
            d_ref[c, t : t + 1, :] = jnp.sum(unscaled * prob_grad, 0, keepdims=True)


def piece_stats(offset, q, g, pair):
    shape = jax.ShapeDtypeStruct((PIECES, TILES, ROWS), F32)
    return pl.pallas_call(
        functools.partial(piece_kernel, offset),
        in_specs=[VMEM] * 4,
        out_specs=[VMEM] * 3,
        out_shape=[shape] * 3,
        compiler_params=pltpu.CompilerParams(vmem_limit_bytes=40 << 20),
        cost_estimate=pl.CostEstimate(flops=(2 if offset == 0 else 3) << 30, bytes_accessed=1 << 10, transcendentals=0),
        name="stats_%d" % offset,
    )(q, g, pair[0], pair[1])


def join_pieces(first_ref, bound_ref, q_ref, g_ref, near_refs, piece_refs, m_ref, l_ref, d_ref, k_all, v_all):
    bounds = bound_ref[...]
    whole = []
    top = jnp.full(bounds.shape, FILL, F32)
    for offset in range(NEAR):
        for c in range(PIECES):
            ok = bounds <= c * PIECE - offset * BLOCK
            part = jnp.where(ok, piece_refs[3 * offset][c], FILL)
            top = jnp.maximum(top, part)
            whole.append((offset, c, ok, part))
    total = jnp.zeros_like(top)
    product = jnp.zeros_like(top)
    for offset, c, ok, part in whole:
        decay = jnp.where(ok, jnp.exp2((part - top) * EXP2_SCALE), 0.0)
        total += piece_refs[3 * offset + 1][c] * decay
        product += piece_refs[3 * offset + 2][c] * decay
    m_ref[...] = top
    l_ref[...] = total
    d_ref[...] = product
    edge = (NEAR - 1) * BLOCK

    @pl.when(first_ref[TILES - 1, 1] > -edge)
    def _():
        for offset in range(NEAR):
            begin = (NEAR - 1 - offset) * BLOCK
            k_all[begin : begin + BLOCK, :] = near_refs[2 * offset][...]
            v_all[begin : begin + BLOCK, :] = near_refs[2 * offset + 1][...]

        def tile(t, carry):
            rows = tile_rows(t)
            one = pl.ds(t, 1)
            bound = bound_ref[one, :]
            token = t * TOKENS + lax.broadcasted_iota(jnp.int32, (1, ROWS), 1) // HEADS

            def piece(j, carry):
                keys = pl.ds(pl.multiple_of(j * PIECE, PIECE), PIECE)
                start = j * PIECE - edge
                scores = dot(k_all[keys, :], q_ref[rows, :], 1, 1)
                key = start + lax.broadcasted_iota(jnp.int32, scores.shape, 0)
                ok = (key >= bound) & (key <= token) & (bound > start)
                scores = jnp.where(ok, scores, FILL)
                prob_grad = dot(v_all[keys, :], g_ref[rows, :], 1, 1)
                before = m_ref[one, :]
                high = jnp.maximum(jnp.max(scores, 0, keepdims=True), before)
                unscaled = jnp.exp2(scores * EXP2_SCALE - high * EXP2_SCALE)
                decay = jnp.exp2((before - high) * EXP2_SCALE)
                m_ref[one, :] = high
                l_ref[one, :] = jnp.sum(unscaled, 0, keepdims=True) + l_ref[one, :] * decay
                d_ref[one, :] = (
                    jnp.sum(unscaled * prob_grad, 0, keepdims=True) + d_ref[one, :] * decay
                )
                return carry

            low = jnp.maximum(first_ref[t, 0] + edge, 0) // PIECE
            high = jnp.where(first_ref[t, 1] > -edge, (first_ref[t, 1] + edge) // PIECE + 1, 0)
            lax.fori_loop(low, high, piece, 0)
            return carry

        lax.fori_loop(0, TILES, tile, 0)


def far_kernel(*refs):
    first_ref, bound_ref, q_ref, g_ref = refs[:4]
    near_refs = refs[4 : 4 + 2 * NEAR]
    k_ref, v_ref = refs[4 + 2 * NEAR : 6 + 2 * NEAR]
    piece_refs = refs[6 + 2 * NEAR : 6 + 5 * NEAR]
    lse_ref, d_ref, dq_ref, pair_ref = refs[6 + 5 * NEAR : 10 + 5 * NEAR]
    key_acc, value_acc, m_ref, l_ref, d_in, k_all, v_all = refs[10 + 5 * NEAR :]
    offset = SPAN - 1
    key_acc[...] = jnp.zeros_like(key_acc)
    value_acc[...] = jnp.zeros_like(value_acc)
    dq_ref[...] = jnp.zeros_like(dq_ref)
    join_pieces(
        first_ref, bound_ref, q_ref, g_ref, near_refs, piece_refs, m_ref, l_ref, d_in, k_all, v_all
    )
    lse_ref[...] = m_ref[...] * EXP2_SCALE + jnp.log2(l_ref[...])
    d_ref[...] = d_in[...] / l_ref[...]

    def visit(t):
        rows = tile_rows(t)
        one = pl.ds(t, 1)
        scores = dot(k_ref[...], q_ref[rows, :], 1, 1)
        scores = masked_scores(scores, bound_ref[one, :], offset, t)
        prob_grad = dot(v_ref[...], g_ref[rows, :], 1, 1)
        before = m_ref[one, :]
        top = jnp.maximum(jnp.max(scores, 0, keepdims=True), before)
        unscaled = jnp.exp2(scores * EXP2_SCALE - top * EXP2_SCALE)
        decay = jnp.exp2((before - top) * EXP2_SCALE)
        total = jnp.sum(unscaled, 0, keepdims=True) + l_ref[one, :] * decay
        product = jnp.sum(unscaled * prob_grad, 0, keepdims=True) + d_in[one, :] * decay
        inverse = 1.0 / total
        row_dot = product * inverse
        lse_ref[one, :] = top * EXP2_SCALE + jnp.log2(total)
        d_ref[one, :] = row_dot
        prob = unscaled * inverse
        score_grad = (prob * (prob_grad - row_dot)).astype(BF16)
        value_acc[...] += dot(prob.astype(BF16), g_ref[rows, :], 1, 0)
        key_acc[...] += dot(score_grad, q_ref[rows, :], 1, 0)
        dq_ref[:, rows] = dot(k_ref[...], score_grad, 0, 0)

    over_tiles(first_ref, offset, visit)
    pair_ref[0] = (key_acc[...] * SCALE).astype(pair_ref.dtype)
    pair_ref[1] = value_acc[...].astype(pair_ref.dtype)


def far_grad(first, bounds, q, g, kv, pieces):
    row = jax.ShapeDtypeStruct((TILES, ROWS), F32)
    operands = [first, bounds, q, g]
    for pair in kv:
        operands += list(pair)
    for piece in pieces:
        operands += list(piece)
    return pl.pallas_call(
        far_kernel,
        in_specs=[SMEM] + [VMEM] * (len(operands) - 1),
        out_specs=[VMEM] * 4,
        out_shape=[
            row,
            row,
            jax.ShapeDtypeStruct((WIDTH, TILES * ROWS), F32),
            jax.ShapeDtypeStruct((2, BLOCK, WIDTH), BF16),
        ],
        scratch_shapes=[pltpu.VMEM((BLOCK, WIDTH), F32)] * 2
        + [pltpu.VMEM((TILES, ROWS), F32)] * 3
        + [pltpu.VMEM((NEAR * BLOCK, WIDTH), BF16)] * 2,
        compiler_params=pltpu.CompilerParams(vmem_limit_bytes=40 << 20),
        cost_estimate=pl.CostEstimate(flops=8 << 30, bytes_accessed=1 << 10, transcendentals=0),
        name="grad_far",
    )(*operands)


def grad_kernel(offset, *refs):
    first_ref, bound_ref, q_ref, g_ref, k_ref, v_ref, m_ref, d_ref = refs[:8]
    dq_in, dq_ref, dk_ref, dv_ref, key_acc, value_acc = refs[8:]
    key_acc[...] = jnp.zeros_like(key_acc)
    value_acc[...] = jnp.zeros_like(value_acc)

    def visit(t):
        rows = tile_rows(t)
        one = pl.ds(t, 1)
        extent = own_extent(t) if offset == 0 else BLOCK
        keys = k_ref[0:extent, :]
        scores = dot(keys, q_ref[rows, :], 1, 1)
        scores = masked_scores(scores, bound_ref[one, :], offset, t)
        prob_grad = dot(v_ref[0:extent, :], g_ref[rows, :], 1, 1)
        prob = jnp.exp2(scores * EXP2_SCALE - m_ref[one, :])
        score_grad = (prob * (prob_grad - d_ref[one, :])).astype(BF16)
        value_acc[0:extent, :] += dot(prob.astype(BF16), g_ref[rows, :], 1, 0)
        key_acc[0:extent, :] += dot(score_grad, q_ref[rows, :], 1, 0)
        part = dot(keys, score_grad, 0, 0)
        if offset == 0:
            dq_ref[rows, :] = jnp.transpose(((dq_in[:, rows] + part) * SCALE).astype(BF16))
        else:
            dq_ref[:, rows] += part

    over_tiles(first_ref, offset, visit)
    dk_ref[...] = key_acc[...] * SCALE
    dv_ref[...] = value_acc[...]


def grad(offset, first, bounds, q, g, pair, lse, row_dot, dq):
    operands = [first, bounds, q, g, pair[0], pair[1], lse, row_dot, dq]
    if offset:
        dq_shape = jax.ShapeDtypeStruct((WIDTH, TILES * ROWS), F32)
    else:
        dq_shape = jax.ShapeDtypeStruct((TILES * ROWS, WIDTH), BF16)
    return pl.pallas_call(
        functools.partial(grad_kernel, offset),
        in_specs=[SMEM] + [VMEM] * (len(operands) - 1),
        out_specs=[VMEM] * 3,
        out_shape=[dq_shape] + [jax.ShapeDtypeStruct((BLOCK, WIDTH), F32)] * 2,
        scratch_shapes=[pltpu.VMEM((BLOCK, WIDTH), F32)] * 2,
        input_output_aliases={8: 0} if offset else {},
        compiler_params=pltpu.CompilerParams(vmem_limit_bytes=40 << 20),
        cost_estimate=pl.CostEstimate(flops=(6 if offset else 5) << 30, bytes_accessed=1 << 10, transcendentals=0),
        name="grad_%d" % offset,
    )(*operands)


def ring(value, steps):
    count = lax.axis_size("ctx")
    return lax.ppermute(value, "ctx", [(s, (s + steps) % count) for s in range(count)])


def pair_swap(value):
    return lax.ppermute(value, "ctx", [(s, s ^ 1) for s in range(lax.axis_size("ctx"))])


def near_and_far(value):
    count = lax.axis_size("ctx")
    return lax.ppermute(
        value, "ctx", [(s, s + 1 if s % 2 == 0 else (s + 3) % count) for s in range(count)]
    )


def local(queries, key_heads, value_head_rows, out_grad, doc_start):
    block_len, head_count, head_width = queries.shape
    ctx = lax.axis_index("ctx")
    member = lax.axis_index("kv")
    members = lax.axis_size("kv")
    q = queries.reshape(block_len * head_count, head_width)
    g = out_grad.reshape(block_len * head_count, head_width)
    k = key_heads.reshape(block_len, head_width)
    v = value_head_rows.reshape(block_len, head_width)

    both = jnp.stack([k, v])
    two = ring(both, 2)
    mixed = near_and_far(both)
    near = piece_stats(0, q, g, (k, v))
    own = jnp.repeat(doc_start - ctx * block_len, head_count)[None, :]
    place = lax.broadcasted_iota(jnp.int32, (members, 1), 0)
    bounds = jnp.where(place == member, own, 0)
    step = 1
    while step < members:
        if step == 4:
            bounds, two = lax.optimization_barrier((bounds, two))
        bounds = bounds + lax.ppermute(bounds, "kv", [(s, s ^ step) for s in range(members)])
        step *= 2
    first = jnp.stack([bounds[:, 0], bounds[:, -1]], 1)

    even = ctx % 2 == 0
    swapped = pair_swap(two)
    one = jnp.where(even, swapped, mixed)
    three = jnp.where(even, mixed, swapped)
    kv = [(k, v)] + [(a[0], a[1]) for a in (one, two, three)]
    pieces = [near] + [piece_stats(offset, q, g, kv[offset]) for offset in range(1, NEAR)]
    lse, row_dot, dq, chain = far_grad(first, bounds, q, g, kv, pieces)
    for offset in (2, 1):
        back = ring(chain, -1)
        dq, dk, dv = grad(offset, first, bounds, q, g, kv[offset], lse, row_dot, dq)
        chain = (jnp.stack([dk, dv]) + back.astype(F32)).astype(BF16)
    back = ring(chain, -1).astype(F32)
    dq, dk, dv = grad(0, first, bounds, q, g, kv[0], lse, row_dot, dq)
    return (
        dq.reshape(queries.shape),
        (dk + back[0]).astype(BF16).reshape(key_heads.shape),
        (dv + back[1]).astype(BF16).reshape(value_head_rows.shape),
    )


def solution(mesh):
    return jax.shard_map(
        local,
        mesh=mesh,
        in_specs=(
            P("ctx", "kv", None),
            P("ctx", "kv", None),
            P("ctx", "kv", None),
            P("ctx", "kv", None),
            P(("ctx", "kv")),
        ),
        out_specs=(P("ctx", "kv", None), P("ctx", "kv", None), P("ctx", "kv", None)),
        check_vma=False,
    )
```

```python
import functools
import math

import jax
import jax.numpy as jnp
from jax import lax
from jax.experimental import pallas as pl
from jax.experimental.pallas import tpu as pltpu
from jax.sharding import PartitionSpec as P

SPAN = 4
BLOCK = 512
HEADS = 8
WIDTH = 128
TILES = 8
ROWS = BLOCK * HEADS // TILES
TOKENS = BLOCK // TILES
SCALE = 1.0 / math.sqrt(WIDTH)
EXP2_SCALE = SCALE * math.log2(math.e)
FILL = -1e30
PIECE = 256
PIECES = BLOCK // PIECE
NEAR = SPAN - 1

VMEM = pl.BlockSpec(memory_space=pltpu.VMEM)
SMEM = pl.BlockSpec(memory_space=pltpu.SMEM)
F32 = jnp.float32
BF16 = jnp.bfloat16


def dot(a, b, ca, cb):
    return lax.dot_general(a, b, (((ca,), (cb,)), ((), ())), preferred_element_type=F32)


def tile_rows(t):
    if isinstance(t, int):
        return pl.ds(t * ROWS, ROWS)
    return pl.ds(pl.multiple_of(t * ROWS, ROWS), ROWS)


def own_extent(t):
    return 128 * ((t * TOKENS + TOKENS - 1) // 128 + 1)


def masked_scores(scores, bounds, offset, t):
    key = lax.broadcasted_iota(jnp.int32, scores.shape, 0) - offset * BLOCK
    if offset:
        return jnp.where(key >= bounds, scores, FILL)
    token = t * TOKENS + lax.broadcasted_iota(jnp.int32, (1, scores.shape[1]), 1) // HEADS
    return jnp.where((key >= bounds) & (key <= token), scores, FILL)


def reached_tiles(first_ref, offset):
    count = jnp.int32(0)
    for t in range(TILES):
        count += (first_ref[t, 0] < (1 - offset) * BLOCK).astype(jnp.int32)
    return count


def over_tiles(first_ref, offset, begin, finish):
    def every():
        held = begin(0)
        for t in range(1, TILES):
            following = begin(t)
            finish(t - 1, *held)
            held = following
        finish(TILES - 1, *held)

    if offset == 0:
        every()
        return
    count = reached_tiles(first_ref, offset)
    pl.when(count == TILES)(every)

    @pl.when(count < TILES)
    def _():
        lax.fori_loop(0, count, lambda t, c: (finish(t, *begin(t)), c)[1], 0)


def piece_kernel(offset, q_ref, g_ref, kv_ref, m_ref, l_ref, d_ref):
    k_ref, v_ref = kv_ref.at[0], kv_ref.at[1]
    if offset == 0:
        m_ref[...] = jnp.full_like(m_ref, FILL)
        l_ref[...] = jnp.zeros_like(l_ref)
        d_ref[...] = jnp.zeros_like(d_ref)
    for t in range(TILES):
        rows = tile_rows(t)
        for c in range(PIECES):
            begin = c * PIECE
            end = begin + PIECE
            if offset == 0:
                end = min(end, own_extent(t))
                if end <= begin:
                    continue
            scores = dot(k_ref[begin:end, :], q_ref[rows, :], 1, 1)
            if offset == 0 and end > t * TOKENS:
                key = begin + lax.broadcasted_iota(jnp.int32, scores.shape, 0)
                token = t * TOKENS + lax.broadcasted_iota(jnp.int32, (1, ROWS), 1) // HEADS
                scores = jnp.where(key <= token, scores, FILL)
            prob_grad = dot(v_ref[begin:end, :], g_ref[rows, :], 1, 1)
            top = jnp.max(scores, 0, keepdims=True)
            unscaled = jnp.exp2(scores * EXP2_SCALE - top * EXP2_SCALE)
            m_ref[c, t : t + 1, :] = top
            l_ref[c, t : t + 1, :] = jnp.sum(unscaled, 0, keepdims=True)
            d_ref[c, t : t + 1, :] = jnp.sum(unscaled * prob_grad, 0, keepdims=True)


def piece_stats(offset, q, g, pair):
    shape = jax.ShapeDtypeStruct((PIECES, TILES, ROWS), F32)
    return pl.pallas_call(
        functools.partial(piece_kernel, offset),
        in_specs=[VMEM] * 3,
        out_specs=[VMEM] * 3,
        out_shape=[shape] * 3,
        compiler_params=pltpu.CompilerParams(vmem_limit_bytes=40 << 20),
        cost_estimate=pl.CostEstimate(flops=(2 if offset == 0 else 3) << 30, bytes_accessed=1 << 10, transcendentals=0),
        name="stats_%d" % offset,
    )(q, g, pair)


def join_pieces(first_ref, bound_ref, q_ref, g_ref, near_refs, piece_refs, m_ref, l_ref, d_ref, k_all, v_all):
    bounds = bound_ref[...]
    whole = []
    top = jnp.full(bounds.shape, FILL, F32)
    for offset in range(NEAR):
        for c in range(PIECES):
            ok = bounds <= c * PIECE - offset * BLOCK
            part = jnp.where(ok, piece_refs[3 * offset][c], FILL)
            top = jnp.maximum(top, part)
            whole.append((offset, c, ok, part))
    total = jnp.zeros_like(top)
    product = jnp.zeros_like(top)
    for offset, c, ok, part in whole:
        decay = jnp.where(ok, jnp.exp2((part - top) * EXP2_SCALE), 0.0)
        total += piece_refs[3 * offset + 1][c] * decay
        product += piece_refs[3 * offset + 2][c] * decay
    m_ref[...] = top
    l_ref[...] = total
    d_ref[...] = product
    edge = (NEAR - 1) * BLOCK

    @pl.when(first_ref[TILES - 1, 1] > -edge)
    def _():
        for offset in range(NEAR):
            begin = (NEAR - 1 - offset) * BLOCK
            k_all[begin : begin + BLOCK, :] = near_refs[offset][0]
            v_all[begin : begin + BLOCK, :] = near_refs[offset][1]

        def tile(t, carry):
            rows = tile_rows(t)
            one = pl.ds(t, 1)
            bound = bound_ref[one, :]
            token = t * TOKENS + lax.broadcasted_iota(jnp.int32, (1, ROWS), 1) // HEADS

            def piece(j, carry):
                start = j * PIECE - edge
                cut = jnp.where((bound > start) & (bound < start + PIECE), 1.0, 0.0)

                @pl.when(jnp.max(cut) > 0.0)
                def _():
                    keys = pl.ds(pl.multiple_of(j * PIECE, PIECE), PIECE)
                    scores = dot(k_all[keys, :], q_ref[rows, :], 1, 1)
                    key = start + lax.broadcasted_iota(jnp.int32, scores.shape, 0)
                    ok = (key >= bound) & (key <= token) & (bound > start)
                    scores = jnp.where(ok, scores, FILL)
                    prob_grad = dot(v_all[keys, :], g_ref[rows, :], 1, 1)
                    before = m_ref[one, :]
                    high = jnp.maximum(jnp.max(scores, 0, keepdims=True), before)
                    unscaled = jnp.exp2(scores * EXP2_SCALE - high * EXP2_SCALE)
                    decay = jnp.exp2((before - high) * EXP2_SCALE)
                    m_ref[one, :] = high
                    l_ref[one, :] = jnp.sum(unscaled, 0, keepdims=True) + l_ref[one, :] * decay
                    d_ref[one, :] = (
                        jnp.sum(unscaled * prob_grad, 0, keepdims=True) + d_ref[one, :] * decay
                    )
                return carry

            low = jnp.maximum(first_ref[t, 0] + edge, 0) // PIECE
            high = jnp.where(first_ref[t, 1] > -edge, (first_ref[t, 1] + edge) // PIECE + 1, 0)
            lax.fori_loop(low, high, piece, 0)
            return carry

        lax.fori_loop(0, TILES, tile, 0)


def far_kernel(*refs):
    first_ref, bound_ref, q_ref, g_ref = refs[:4]
    near_refs = refs[4 : 4 + NEAR]
    k_ref, v_ref = refs[4 + NEAR].at[0], refs[4 + NEAR].at[1]
    piece_refs = refs[5 + NEAR : 5 + 4 * NEAR]
    lse_ref, d_ref, dq_ref, pair_ref = refs[5 + 4 * NEAR : 9 + 4 * NEAR]
    key_acc, value_acc, m_ref, l_ref, d_in, k_all, v_all = refs[9 + 4 * NEAR :]
    offset = SPAN - 1
    key_acc[...] = jnp.zeros_like(key_acc)
    value_acc[...] = jnp.zeros_like(value_acc)
    dq_ref[...] = jnp.zeros_like(dq_ref)
    join_pieces(
        first_ref, bound_ref, q_ref, g_ref, near_refs, piece_refs, m_ref, l_ref, d_in, k_all, v_all
    )
    lse_ref[...] = m_ref[...] * EXP2_SCALE + jnp.log2(l_ref[...])
    d_ref[...] = d_in[...] / l_ref[...]

    def begin(t):
        rows = tile_rows(t)
        one = pl.ds(t, 1)
        scores = dot(k_ref[...], q_ref[rows, :], 1, 1)
        scores = masked_scores(scores, bound_ref[one, :], offset, t)
        prob_grad = dot(v_ref[...], g_ref[rows, :], 1, 1)
        before = m_ref[one, :]
        top = jnp.maximum(jnp.max(scores, 0, keepdims=True), before)
        unscaled = jnp.exp2(scores * EXP2_SCALE - top * EXP2_SCALE)
        decay = jnp.exp2((before - top) * EXP2_SCALE)
        total = jnp.sum(unscaled, 0, keepdims=True) + l_ref[one, :] * decay
        product = jnp.sum(unscaled * prob_grad, 0, keepdims=True) + d_in[one, :] * decay
        inverse = 1.0 / total
        row_dot = product * inverse
        lse_ref[one, :] = top * EXP2_SCALE + jnp.log2(total)
        d_ref[one, :] = row_dot
        prob = unscaled * inverse
        score_grad = (prob * (prob_grad - row_dot)).astype(BF16)
        return prob.astype(BF16), score_grad

    def finish(t, prob, score_grad):
        rows = tile_rows(t)
        value_acc[...] += dot(prob, g_ref[rows, :], 1, 0)
        key_acc[...] += dot(score_grad, q_ref[rows, :], 1, 0)
        dq_ref[:, rows] = dot(k_ref[...], score_grad, 0, 0)

    over_tiles(first_ref, offset, begin, finish)
    pair_ref[0] = (key_acc[...] * SCALE).astype(pair_ref.dtype)
    pair_ref[1] = value_acc[...].astype(pair_ref.dtype)


def far_grad(first, bounds, q, g, kv, pieces):
    row = jax.ShapeDtypeStruct((TILES, ROWS), F32)
    operands = [first, bounds, q, g] + kv
    for piece in pieces:
        operands += list(piece)
    return pl.pallas_call(
        far_kernel,
        in_specs=[SMEM] + [VMEM] * (len(operands) - 1),
        out_specs=[VMEM] * 4,
        out_shape=[
            row,
            row,
            jax.ShapeDtypeStruct((WIDTH, TILES * ROWS), F32),
            jax.ShapeDtypeStruct((2, BLOCK, WIDTH), BF16),
        ],
        scratch_shapes=[pltpu.VMEM((BLOCK, WIDTH), F32)] * 2
        + [pltpu.VMEM((TILES, ROWS), F32)] * 3
        + [pltpu.VMEM((NEAR * BLOCK, WIDTH), BF16)] * 2,
        compiler_params=pltpu.CompilerParams(vmem_limit_bytes=40 << 20),
        cost_estimate=pl.CostEstimate(flops=8 << 30, bytes_accessed=1 << 10, transcendentals=0),
        name="grad_far",
    )(*operands)


def grad_kernel(offset, *refs):
    first_ref, bound_ref, q_ref, g_ref, kv_ref, m_ref, d_ref, dq_in = refs[:8]
    k_ref, v_ref = kv_ref.at[0], kv_ref.at[1]
    dq_ref, pair_ref, key_acc, value_acc = refs[8:]
    key_acc[...] = jnp.zeros_like(key_acc)
    value_acc[...] = jnp.zeros_like(value_acc)

    def begin(t):
        rows = tile_rows(t)
        one = pl.ds(t, 1)
        extent = own_extent(t) if offset == 0 else BLOCK
        scores = dot(k_ref[0:extent, :], q_ref[rows, :], 1, 1)
        scores = masked_scores(scores, bound_ref[one, :], offset, t)
        prob_grad = dot(v_ref[0:extent, :], g_ref[rows, :], 1, 1)
        prob = jnp.exp2(scores * EXP2_SCALE - m_ref[one, :])
        score_grad = (prob * (prob_grad - d_ref[one, :])).astype(BF16)
        return prob.astype(BF16), score_grad

    def finish(t, prob, score_grad):
        rows = tile_rows(t)
        extent = own_extent(t) if offset == 0 else BLOCK
        value_acc[0:extent, :] += dot(prob, g_ref[rows, :], 1, 0)
        key_acc[0:extent, :] += dot(score_grad, q_ref[rows, :], 1, 0)
        part = dot(k_ref[0:extent, :], score_grad, 0, 0)
        if offset == 0:
            dq_ref[rows, :] = jnp.transpose(((dq_in[:, rows] + part) * SCALE).astype(BF16))
        else:
            dq_ref[:, rows] += part

    over_tiles(first_ref, offset, begin, finish)
    pair_ref[0] = key_acc[...] * SCALE
    pair_ref[1] = value_acc[...]


def grad(offset, first, bounds, q, g, pair, lse, row_dot, dq):
    operands = [first, bounds, q, g, pair, lse, row_dot, dq]
    if offset:
        dq_shape = jax.ShapeDtypeStruct((WIDTH, TILES * ROWS), F32)
    else:
        dq_shape = jax.ShapeDtypeStruct((TILES * ROWS, WIDTH), BF16)
    return pl.pallas_call(
        functools.partial(grad_kernel, offset),
        in_specs=[SMEM] + [VMEM] * (len(operands) - 1),
        out_specs=[VMEM] * 2,
        out_shape=[dq_shape] + [jax.ShapeDtypeStruct((2, BLOCK, WIDTH), F32)],
        scratch_shapes=[pltpu.VMEM((BLOCK, WIDTH), F32)] * 2,
        input_output_aliases={7: 0} if offset else {},
        compiler_params=pltpu.CompilerParams(vmem_limit_bytes=40 << 20),
        cost_estimate=pl.CostEstimate(flops=(6 if offset else 5) << 30, bytes_accessed=1 << 10, transcendentals=0),
        name="grad_%d" % offset,
    )(*operands)


def ring(value, steps):
    count = lax.axis_size("ctx")
    return lax.ppermute(value, "ctx", [(s, (s + steps) % count) for s in range(count)])


def pair_swap(value):
    return lax.ppermute(value, "ctx", [(s, s ^ 1) for s in range(lax.axis_size("ctx"))])


def near_and_far(value):
    count = lax.axis_size("ctx")
    return lax.ppermute(
        value, "ctx", [(s, s + 1 if s % 2 == 0 else (s + 3) % count) for s in range(count)]
    )


def local(queries, key_heads, value_head_rows, out_grad, doc_start):
    block_len, head_count, head_width = queries.shape
    ctx = lax.axis_index("ctx")
    member = lax.axis_index("kv")
    members = lax.axis_size("kv")
    q = queries.reshape(block_len * head_count, head_width)
    g = out_grad.reshape(block_len * head_count, head_width)
    k = key_heads.reshape(block_len, head_width)
    v = value_head_rows.reshape(block_len, head_width)

    both = jnp.stack([k, v])
    two = ring(both, 2)
    mixed = near_and_far(both)
    near = piece_stats(0, q, g, both)
    own = jnp.repeat(doc_start - ctx * block_len, head_count)[None, :]
    place = lax.broadcasted_iota(jnp.int32, (members, 1), 0)
    bounds = jnp.where(place == member, own, 0)
    step = 1
    while step < members:
        if step == 4:
            bounds, two = lax.optimization_barrier((bounds, two))
        bounds = bounds + lax.ppermute(bounds, "kv", [(s, s ^ step) for s in range(members)])
        step *= 2
    first = jnp.stack([bounds[:, 0], bounds[:, -1]], 1)

    even = ctx % 2 == 0
    swapped = pair_swap(two)
    one = jnp.where(even, swapped, mixed)
    three = jnp.where(even, mixed, swapped)
    kv = [both, one, two, three]
    pieces = [near] + [piece_stats(offset, q, g, kv[offset]) for offset in range(1, NEAR)]
    lse, row_dot, dq, chain = far_grad(first, bounds, q, g, kv, pieces)
    for offset in (2, 1):
        back = ring(chain, -1)
        dq, part = grad(offset, first, bounds, q, g, kv[offset], lse, row_dot, dq)
        chain = (part + back.astype(F32)).astype(BF16)
    back = ring(chain, -1)
    dq, part = grad(0, first, bounds, q, g, kv[0], lse, row_dot, dq)
    return (
        dq.reshape(queries.shape),
        (part[0] + back[0].astype(F32)).astype(BF16).reshape(key_heads.shape),
        (part[1] + back[1].astype(F32)).astype(BF16).reshape(value_head_rows.shape),
    )


def solution(mesh):
    return jax.shard_map(
        local,
        mesh=mesh,
        in_specs=(
            P("ctx", "kv", None),
            P("ctx", "kv", None),
            P("ctx", "kv", None),
            P("ctx", "kv", None),
            P(("ctx", "kv")),
        ),
        out_specs=(P("ctx", "kv", None), P("ctx", "kv", None), P("ctx", "kv", None)),
        check_vma=False,
    )
```

```python
import functools
import math

import jax
import jax.numpy as jnp
from jax import lax
from jax.experimental import pallas as pl
from jax.experimental.pallas import tpu as pltpu
from jax.sharding import PartitionSpec as P

SPAN = 4
BLOCK = 512
HEADS = 8
WIDTH = 128
TILES = 8
ROWS = BLOCK * HEADS // TILES
TOKENS = BLOCK // TILES
SCALE = 1.0 / math.sqrt(WIDTH)
EXP2_SCALE = SCALE * math.log2(math.e)
FILL = -1e30
PIECE = 256
PIECES = BLOCK // PIECE
NEAR = SPAN - 1

VMEM = pl.BlockSpec(memory_space=pltpu.VMEM)
SMEM = pl.BlockSpec(memory_space=pltpu.SMEM)
F32 = jnp.float32
BF16 = jnp.bfloat16


def dot(a, b, ca, cb):
    return lax.dot_general(a, b, (((ca,), (cb,)), ((), ())), preferred_element_type=F32)


def tile_rows(t):
    if isinstance(t, int):
        return pl.ds(t * ROWS, ROWS)
    return pl.ds(pl.multiple_of(t * ROWS, ROWS), ROWS)


def own_extent(t):
    return 128 * ((t * TOKENS + TOKENS - 1) // 128 + 1)


def masked_scores(scores, bounds, offset, t):
    key = lax.broadcasted_iota(jnp.int32, scores.shape, 0) - offset * BLOCK
    if offset:
        return jnp.where(key >= bounds, scores, FILL)
    token = t * TOKENS + lax.broadcasted_iota(jnp.int32, (1, scores.shape[1]), 1) // HEADS
    return jnp.where((key >= bounds) & (key <= token), scores, FILL)


def reached_tiles(first_ref, offset):
    count = jnp.int32(0)
    for t in range(TILES):
        count += (first_ref[t, 0] < (1 - offset) * BLOCK).astype(jnp.int32)
    return count


def over_tiles(first_ref, offset, begin, finish):
    def every():
        held = begin(0)
        for t in range(1, TILES):
            following = begin(t)
            finish(t - 1, *held)
            held = following
        finish(TILES - 1, *held)

    if offset == 0:
        every()
        return
    count = reached_tiles(first_ref, offset)
    pl.when(count == TILES)(every)

    @pl.when(count < TILES)
    def _():
        lax.fori_loop(0, count, lambda t, c: (finish(t, *begin(t)), c)[1], 0)


def piece_kernel(offset, q_ref, g_ref, kv_ref, m_ref, l_ref, d_ref):
    k_ref, v_ref = kv_ref.at[0], kv_ref.at[1]
    if offset == 0:
        m_ref[...] = jnp.full_like(m_ref, FILL)
        l_ref[...] = jnp.zeros_like(l_ref)
        d_ref[...] = jnp.zeros_like(d_ref)
    steps = []
    for t in range(TILES):
        for c in range(PIECES):
            end = (c + 1) * PIECE
            if offset == 0:
                end = min(end, own_extent(t))
            if end > c * PIECE:
                steps.append((t, c, c * PIECE, end))

    def begin(t, c, start, end):
        rows = tile_rows(t)
        scores = dot(k_ref[start:end, :], q_ref[rows, :], 1, 1)
        if offset == 0 and end > t * TOKENS:
            key = start + lax.broadcasted_iota(jnp.int32, scores.shape, 0)
            token = t * TOKENS + lax.broadcasted_iota(jnp.int32, (1, ROWS), 1) // HEADS
            scores = jnp.where(key <= token, scores, FILL)
        return scores, jnp.max(scores, 0, keepdims=True)

    def finish(t, c, start, end, scores, top):
        prob_grad = dot(v_ref[start:end, :], g_ref[tile_rows(t), :], 1, 1)
        unscaled = jnp.exp2(scores * EXP2_SCALE - top * EXP2_SCALE)
        m_ref[c, t : t + 1, :] = top
        l_ref[c, t : t + 1, :] = jnp.sum(unscaled, 0, keepdims=True)
        d_ref[c, t : t + 1, :] = jnp.sum(unscaled * prob_grad, 0, keepdims=True)

    held = begin(*steps[0])
    for place in range(1, len(steps)):
        following = begin(*steps[place])
        finish(*steps[place - 1], *held)
        held = following
    finish(*steps[-1], *held)


def piece_stats(offset, q, g, pair):
    shape = jax.ShapeDtypeStruct((PIECES, TILES, ROWS), F32)
    return pl.pallas_call(
        functools.partial(piece_kernel, offset),
        in_specs=[VMEM] * 3,
        out_specs=[VMEM] * 3,
        out_shape=[shape] * 3,
        compiler_params=pltpu.CompilerParams(vmem_limit_bytes=40 << 20),
        cost_estimate=pl.CostEstimate(flops=(2 if offset == 0 else 3) << 30, bytes_accessed=1 << 10, transcendentals=0),
        name="stats_%d" % offset,
    )(q, g, pair)


def join_pieces(first_ref, bound_ref, q_ref, g_ref, near_refs, piece_refs, m_ref, l_ref, d_ref, k_all, v_all):
    bounds = bound_ref[...]
    whole = []
    top = jnp.full(bounds.shape, FILL, F32)
    for offset in range(NEAR):
        for c in range(PIECES):
            ok = bounds <= c * PIECE - offset * BLOCK
            part = jnp.where(ok, piece_refs[3 * offset][c], FILL)
            top = jnp.maximum(top, part)
            whole.append((offset, c, ok, part))
    total = jnp.zeros_like(top)
    product = jnp.zeros_like(top)
    for offset, c, ok, part in whole:
        decay = jnp.where(ok, jnp.exp2((part - top) * EXP2_SCALE), 0.0)
        total += piece_refs[3 * offset + 1][c] * decay
        product += piece_refs[3 * offset + 2][c] * decay
    m_ref[...] = top
    l_ref[...] = total
    d_ref[...] = product
    edge = (NEAR - 1) * BLOCK

    @pl.when(first_ref[TILES - 1, 1] > -edge)
    def _():
        for offset in range(NEAR):
            begin = (NEAR - 1 - offset) * BLOCK
            k_all[begin : begin + BLOCK, :] = near_refs[offset][0]
            v_all[begin : begin + BLOCK, :] = near_refs[offset][1]

        def tile(t, carry):
            rows = tile_rows(t)
            one = pl.ds(t, 1)
            bound = bound_ref[one, :]
            token = t * TOKENS + lax.broadcasted_iota(jnp.int32, (1, ROWS), 1) // HEADS

            def piece(j, carry):
                start = j * PIECE - edge
                cut = jnp.where((bound > start) & (bound < start + PIECE), 1.0, 0.0)

                @pl.when(jnp.max(cut) > 0.0)
                def _():
                    keys = pl.ds(pl.multiple_of(j * PIECE, PIECE), PIECE)
                    scores = dot(k_all[keys, :], q_ref[rows, :], 1, 1)
                    key = start + lax.broadcasted_iota(jnp.int32, scores.shape, 0)
                    ok = (key >= bound) & (key <= token) & (bound > start)
                    scores = jnp.where(ok, scores, FILL)
                    prob_grad = dot(v_all[keys, :], g_ref[rows, :], 1, 1)
                    before = m_ref[one, :]
                    high = jnp.maximum(jnp.max(scores, 0, keepdims=True), before)
                    unscaled = jnp.exp2(scores * EXP2_SCALE - high * EXP2_SCALE)
                    decay = jnp.exp2((before - high) * EXP2_SCALE)
                    m_ref[one, :] = high
                    l_ref[one, :] = jnp.sum(unscaled, 0, keepdims=True) + l_ref[one, :] * decay
                    d_ref[one, :] = (
                        jnp.sum(unscaled * prob_grad, 0, keepdims=True) + d_ref[one, :] * decay
                    )
                return carry

            low = jnp.maximum(first_ref[t, 0] + edge, 0) // PIECE
            high = jnp.where(first_ref[t, 1] > -edge, (first_ref[t, 1] + edge) // PIECE + 1, 0)
            lax.fori_loop(low, high, piece, 0)
            return carry

        lax.fori_loop(0, TILES, tile, 0)


def far_kernel(*refs):
    first_ref, bound_ref, q_ref, g_ref = refs[:4]
    near_refs = refs[4 : 4 + NEAR]
    k_ref, v_ref = refs[4 + NEAR].at[0], refs[4 + NEAR].at[1]
    piece_refs = refs[5 + NEAR : 5 + 4 * NEAR]
    lse_ref, d_ref, dq_ref, pair_ref = refs[5 + 4 * NEAR : 9 + 4 * NEAR]
    key_acc, value_acc, m_ref, l_ref, d_in, k_all, v_all = refs[9 + 4 * NEAR :]
    offset = SPAN - 1
    key_acc[...] = jnp.zeros_like(key_acc)
    value_acc[...] = jnp.zeros_like(value_acc)
    dq_ref[...] = jnp.zeros_like(dq_ref)
    join_pieces(
        first_ref, bound_ref, q_ref, g_ref, near_refs, piece_refs, m_ref, l_ref, d_in, k_all, v_all
    )
    lse_ref[...] = m_ref[...] * EXP2_SCALE + jnp.log2(l_ref[...])
    d_ref[...] = d_in[...] / l_ref[...]

    def begin(t):
        rows = tile_rows(t)
        one = pl.ds(t, 1)
        scores = dot(k_ref[...], q_ref[rows, :], 1, 1)
        scores = masked_scores(scores, bound_ref[one, :], offset, t)
        prob_grad = dot(v_ref[...], g_ref[rows, :], 1, 1)
        before = m_ref[one, :]
        top = jnp.maximum(jnp.max(scores, 0, keepdims=True), before)
        unscaled = jnp.exp2(scores * EXP2_SCALE - top * EXP2_SCALE)
        decay = jnp.exp2((before - top) * EXP2_SCALE)
        total = jnp.sum(unscaled, 0, keepdims=True) + l_ref[one, :] * decay
        product = jnp.sum(unscaled * prob_grad, 0, keepdims=True) + d_in[one, :] * decay
        inverse = 1.0 / total
        row_dot = product * inverse
        lse_ref[one, :] = top * EXP2_SCALE + jnp.log2(total)
        d_ref[one, :] = row_dot
        prob = unscaled * inverse
        score_grad = (prob * (prob_grad - row_dot)).astype(BF16)
        return prob.astype(BF16), score_grad

    def finish(t, prob, score_grad):
        rows = tile_rows(t)
        value_acc[...] += dot(prob, g_ref[rows, :], 1, 0)
        key_acc[...] += dot(score_grad, q_ref[rows, :], 1, 0)
        dq_ref[:, rows] = dot(k_ref[...], score_grad, 0, 0)

    over_tiles(first_ref, offset, begin, finish)
    pair_ref[0] = (key_acc[...] * SCALE).astype(pair_ref.dtype)
    pair_ref[1] = value_acc[...].astype(pair_ref.dtype)


def far_grad(first, bounds, q, g, kv, pieces):
    row = jax.ShapeDtypeStruct((TILES, ROWS), F32)
    operands = [first, bounds, q, g] + kv
    for piece in pieces:
        operands += list(piece)
    return pl.pallas_call(
        far_kernel,
        in_specs=[SMEM] + [VMEM] * (len(operands) - 1),
        out_specs=[VMEM] * 4,
        out_shape=[
            row,
            row,
            jax.ShapeDtypeStruct((WIDTH, TILES * ROWS), F32),
            jax.ShapeDtypeStruct((2, BLOCK, WIDTH), BF16),
        ],
        scratch_shapes=[pltpu.VMEM((BLOCK, WIDTH), F32)] * 2
        + [pltpu.VMEM((TILES, ROWS), F32)] * 3
        + [pltpu.VMEM((NEAR * BLOCK, WIDTH), BF16)] * 2,
        compiler_params=pltpu.CompilerParams(vmem_limit_bytes=40 << 20),
        cost_estimate=pl.CostEstimate(flops=8 << 30, bytes_accessed=1 << 10, transcendentals=0),
        name="grad_far",
    )(*operands)


def grad_kernel(offset, *refs):
    first_ref, bound_ref, q_ref, g_ref, kv_ref, m_ref, d_ref, dq_in = refs[:8]
    k_ref, v_ref = kv_ref.at[0], kv_ref.at[1]
    dq_ref, pair_ref, key_acc, value_acc = refs[8:]
    key_acc[...] = jnp.zeros_like(key_acc)
    value_acc[...] = jnp.zeros_like(value_acc)

    def begin(t):
        rows = tile_rows(t)
        one = pl.ds(t, 1)
        extent = own_extent(t) if offset == 0 else BLOCK
        scores = dot(k_ref[0:extent, :], q_ref[rows, :], 1, 1)
        scores = masked_scores(scores, bound_ref[one, :], offset, t)
        prob_grad = dot(v_ref[0:extent, :], g_ref[rows, :], 1, 1)
        prob = jnp.exp2(scores * EXP2_SCALE - m_ref[one, :])
        score_grad = (prob * (prob_grad - d_ref[one, :])).astype(BF16)
        return prob.astype(BF16), score_grad

    def finish(t, prob, score_grad):
        rows = tile_rows(t)
        extent = own_extent(t) if offset == 0 else BLOCK
        value_acc[0:extent, :] += dot(prob, g_ref[rows, :], 1, 0)
        key_acc[0:extent, :] += dot(score_grad, q_ref[rows, :], 1, 0)
        part = dot(k_ref[0:extent, :], score_grad, 0, 0)
        if offset == 0:
            dq_ref[rows, :] = jnp.transpose(((dq_in[:, rows] + part) * SCALE).astype(BF16))
        else:
            dq_ref[:, rows] += part

    over_tiles(first_ref, offset, begin, finish)
    pair_ref[0] = key_acc[...] * SCALE
    pair_ref[1] = value_acc[...]


def grad(offset, first, bounds, q, g, pair, lse, row_dot, dq):
    operands = [first, bounds, q, g, pair, lse, row_dot, dq]
    if offset:
        dq_shape = jax.ShapeDtypeStruct((WIDTH, TILES * ROWS), F32)
    else:
        dq_shape = jax.ShapeDtypeStruct((TILES * ROWS, WIDTH), BF16)
    return pl.pallas_call(
        functools.partial(grad_kernel, offset),
        in_specs=[SMEM] + [VMEM] * (len(operands) - 1),
        out_specs=[VMEM] * 2,
        out_shape=[dq_shape] + [jax.ShapeDtypeStruct((2, BLOCK, WIDTH), F32)],
        scratch_shapes=[pltpu.VMEM((BLOCK, WIDTH), F32)] * 2,
        input_output_aliases={7: 0} if offset else {},
        compiler_params=pltpu.CompilerParams(vmem_limit_bytes=40 << 20),
        cost_estimate=pl.CostEstimate(flops=(6 if offset else 5) << 30, bytes_accessed=1 << 10, transcendentals=0),
        name="grad_%d" % offset,
    )(*operands)


def ring(value, steps):
    count = lax.axis_size("ctx")
    return lax.ppermute(value, "ctx", [(s, (s + steps) % count) for s in range(count)])


def pair_swap(value):
    return lax.ppermute(value, "ctx", [(s, s ^ 1) for s in range(lax.axis_size("ctx"))])


def near_and_far(value):
    count = lax.axis_size("ctx")
    return lax.ppermute(
        value, "ctx", [(s, s + 1 if s % 2 == 0 else (s + 3) % count) for s in range(count)]
    )


def local(queries, key_heads, value_head_rows, out_grad, doc_start):
    block_len, head_count, head_width = queries.shape
    ctx = lax.axis_index("ctx")
    member = lax.axis_index("kv")
    members = lax.axis_size("kv")
    q = queries.reshape(block_len * head_count, head_width)
    g = out_grad.reshape(block_len * head_count, head_width)
    k = key_heads.reshape(block_len, head_width)
    v = value_head_rows.reshape(block_len, head_width)

    both = jnp.stack([k, v])
    two = ring(both, 2)
    mixed = near_and_far(both)
    near = piece_stats(0, q, g, both)
    own = jnp.repeat(doc_start - ctx * block_len, head_count)[None, :]
    place = lax.broadcasted_iota(jnp.int32, (members, 1), 0)
    bounds = jnp.where(place == member, own, 0)
    step = 1
    while step < members:
        if step == 4:
            bounds, two = lax.optimization_barrier((bounds, two))
        bounds = bounds + lax.ppermute(bounds, "kv", [(s, s ^ step) for s in range(members)])
        step *= 2
    first = jnp.stack([bounds[:, 0], bounds[:, -1]], 1)

    even = ctx % 2 == 0
    swapped = pair_swap(two)
    one = jnp.where(even, swapped, mixed)
    three = jnp.where(even, mixed, swapped)
    kv = [both, one, two, three]
    pieces = [near] + [piece_stats(offset, q, g, kv[offset]) for offset in range(1, NEAR)]
    lse, row_dot, dq, chain = far_grad(first, bounds, q, g, kv, pieces)
    for offset in (2, 1):
        back = ring(chain, -1)
        dq, part = grad(offset, first, bounds, q, g, kv[offset], lse, row_dot, dq)
        chain = (part + back.astype(F32)).astype(BF16)
    back = ring(chain, -1)
    dq, part = grad(0, first, bounds, q, g, kv[0], lse, row_dot, dq)
    return (
        dq.reshape(queries.shape),
        (part[0] + back[0].astype(F32)).astype(BF16).reshape(key_heads.shape),
        (part[1] + back[1].astype(F32)).astype(BF16).reshape(value_head_rows.shape),
    )


def solution(mesh):
    return jax.shard_map(
        local,
        mesh=mesh,
        in_specs=(
            P("ctx", "kv", None),
            P("ctx", "kv", None),
            P("ctx", "kv", None),
            P("ctx", "kv", None),
            P(("ctx", "kv")),
        ),
        out_specs=(P("ctx", "kv", None), P("ctx", "kv", None), P("ctx", "kv", None)),
        check_vma=False,
    )
```

```python
import functools
import math

import jax
import jax.numpy as jnp
from jax import lax
from jax.experimental import pallas as pl
from jax.experimental.pallas import tpu as pltpu
from jax.sharding import PartitionSpec as P

SPAN = 4
BLOCK = 512
HEADS = 8
WIDTH = 128
TILES = 8
ROWS = BLOCK * HEADS // TILES
TOKENS = BLOCK // TILES
SCALE = 1.0 / math.sqrt(WIDTH)
EXP2_SCALE = SCALE * math.log2(math.e)
FILL = -1e30
PIECE = 256
PIECES = BLOCK // PIECE
NEAR = SPAN - 1

VMEM = pl.BlockSpec(memory_space=pltpu.VMEM)
SMEM = pl.BlockSpec(memory_space=pltpu.SMEM)
F32 = jnp.float32
BF16 = jnp.bfloat16


def dot(a, b, ca, cb):
    return lax.dot_general(a, b, (((ca,), (cb,)), ((), ())), preferred_element_type=F32)


def tile_rows(t):
    if isinstance(t, int):
        return pl.ds(t * ROWS, ROWS)
    return pl.ds(pl.multiple_of(t * ROWS, ROWS), ROWS)


def own_extent(t):
    return 128 * ((t * TOKENS + TOKENS - 1) // 128 + 1)


def masked_scores(scores, bounds, offset, t):
    key = lax.broadcasted_iota(jnp.int32, scores.shape, 0) - offset * BLOCK
    if offset:
        return jnp.where(key >= bounds, scores, FILL)
    token = t * TOKENS + lax.broadcasted_iota(jnp.int32, (1, scores.shape[1]), 1) // HEADS
    return jnp.where((key >= bounds) & (key <= token), scores, FILL)


def reached_tiles(first_ref, offset):
    count = jnp.int32(0)
    for t in range(TILES):
        count += (first_ref[t, 0] < (1 - offset) * BLOCK).astype(jnp.int32)
    return count


def over_tiles(first_ref, offset, begin, finish):
    def every():
        held = begin(0)
        for t in range(1, TILES):
            following = begin(t)
            finish(t - 1, *held)
            held = following
        finish(TILES - 1, *held)

    if offset == 0:
        every()
        return
    count = reached_tiles(first_ref, offset)
    pl.when(count == TILES)(every)

    @pl.when(count < TILES)
    def _():
        lax.fori_loop(0, count, lambda t, c: (finish(t, *begin(t)), c)[1], 0)


def piece_kernel(offset, q_ref, g_ref, kv_ref, m_ref, l_ref, d_ref):
    k_ref, v_ref = kv_ref.at[0], kv_ref.at[1]
    if offset == 0:
        m_ref[...] = jnp.full_like(m_ref, FILL)
        l_ref[...] = jnp.zeros_like(l_ref)
        d_ref[...] = jnp.zeros_like(d_ref)
    steps = []
    for t in range(TILES):
        for c in range(PIECES):
            end = (c + 1) * PIECE
            if offset == 0:
                end = min(end, own_extent(t))
            if end > c * PIECE:
                steps.append((t, c, c * PIECE, end))

    def begin(t, c, start, end):
        rows = tile_rows(t)
        scores = dot(k_ref[start:end, :], q_ref[rows, :], 1, 1)
        if offset == 0 and end > t * TOKENS:
            key = start + lax.broadcasted_iota(jnp.int32, scores.shape, 0)
            token = t * TOKENS + lax.broadcasted_iota(jnp.int32, (1, ROWS), 1) // HEADS
            scores = jnp.where(key <= token, scores, FILL)
        return scores, jnp.max(scores, 0, keepdims=True)

    def finish(t, c, start, end, scores, top):
        prob_grad = dot(v_ref[start:end, :], g_ref[tile_rows(t), :], 1, 1)
        unscaled = jnp.exp2(scores * EXP2_SCALE - top * EXP2_SCALE)
        m_ref[c, t : t + 1, :] = top
        l_ref[c, t : t + 1, :] = jnp.sum(unscaled, 0, keepdims=True)
        d_ref[c, t : t + 1, :] = jnp.sum(unscaled * prob_grad, 0, keepdims=True)

    held = begin(*steps[0])
    for place in range(1, len(steps)):
        following = begin(*steps[place])
        finish(*steps[place - 1], *held)
        held = following
    finish(*steps[-1], *held)


def piece_stats(offset, q, g, pair):
    shape = jax.ShapeDtypeStruct((PIECES, TILES, ROWS), F32)
    return pl.pallas_call(
        functools.partial(piece_kernel, offset),
        in_specs=[VMEM] * 3,
        out_specs=[VMEM] * 3,
        out_shape=[shape] * 3,
        compiler_params=pltpu.CompilerParams(vmem_limit_bytes=40 << 20),
        cost_estimate=pl.CostEstimate(flops=(2 if offset == 0 else 3) << 30, bytes_accessed=1 << 10, transcendentals=0),
        name="stats_%d" % offset,
    )(q, g, pair)


def join_pieces(first_ref, bound_ref, q_ref, g_ref, near_refs, piece_refs, m_ref, l_ref, d_ref, k_all, v_all):
    bounds = bound_ref[...]
    whole = []
    top = jnp.full(bounds.shape, FILL, F32)
    for offset in range(NEAR):
        for c in range(PIECES):
            ok = bounds <= c * PIECE - offset * BLOCK
            part = jnp.where(ok, piece_refs[3 * offset][c], FILL)
            top = jnp.maximum(top, part)
            whole.append((offset, c, ok, part))
    total = jnp.zeros_like(top)
    product = jnp.zeros_like(top)
    for offset, c, ok, part in whole:
        decay = jnp.where(ok, jnp.exp2((part - top) * EXP2_SCALE), 0.0)
        total += piece_refs[3 * offset + 1][c] * decay
        product += piece_refs[3 * offset + 2][c] * decay
    m_ref[...] = top
    l_ref[...] = total
    d_ref[...] = product
    edge = (NEAR - 1) * BLOCK

    @pl.when(first_ref[TILES - 1, 1] > -edge)
    def _():
        for offset in range(NEAR):
            begin = (NEAR - 1 - offset) * BLOCK
            k_all[begin : begin + BLOCK, :] = near_refs[offset][0]
            v_all[begin : begin + BLOCK, :] = near_refs[offset][1]

        def tile(t, carry):
            rows = tile_rows(t)
            one = pl.ds(t, 1)
            bound = bound_ref[one, :]
            token = t * TOKENS + lax.broadcasted_iota(jnp.int32, (1, ROWS), 1) // HEADS

            def piece(j, carry):
                start = j * PIECE - edge
                cut = jnp.where((bound > start) & (bound < start + PIECE), 1.0, 0.0)

                @pl.when(jnp.max(cut) > 0.0)
                def _():
                    keys = pl.ds(pl.multiple_of(j * PIECE, PIECE), PIECE)
                    scores = dot(k_all[keys, :], q_ref[rows, :], 1, 1)
                    key = start + lax.broadcasted_iota(jnp.int32, scores.shape, 0)
                    ok = (key >= bound) & (key <= token) & (bound > start)
                    scores = jnp.where(ok, scores, FILL)
                    prob_grad = dot(v_all[keys, :], g_ref[rows, :], 1, 1)
                    before = m_ref[one, :]
                    high = jnp.maximum(jnp.max(scores, 0, keepdims=True), before)
                    unscaled = jnp.exp2(scores * EXP2_SCALE - high * EXP2_SCALE)
                    decay = jnp.exp2((before - high) * EXP2_SCALE)
                    m_ref[one, :] = high
                    l_ref[one, :] = jnp.sum(unscaled, 0, keepdims=True) + l_ref[one, :] * decay
                    d_ref[one, :] = (
                        jnp.sum(unscaled * prob_grad, 0, keepdims=True) + d_ref[one, :] * decay
                    )
                return carry

            low = jnp.maximum(first_ref[t, 0] + edge, 0) // PIECE
            high = jnp.where(first_ref[t, 1] > -edge, (first_ref[t, 1] + edge) // PIECE + 1, 0)
            lax.fori_loop(low, high, piece, 0)
            return carry

        lax.fori_loop(0, TILES, tile, 0)


def far_kernel(*refs):
    first_ref, bound_ref, q_ref, g_ref = refs[:4]
    near_refs = refs[4 : 4 + NEAR]
    k_ref, v_ref = refs[4 + NEAR].at[0], refs[4 + NEAR].at[1]
    piece_refs = refs[5 + NEAR : 5 + 4 * NEAR]
    lse_ref, d_ref, dq_ref, pair_ref = refs[5 + 4 * NEAR : 9 + 4 * NEAR]
    key_acc, value_acc, m_ref, l_ref, d_in, k_all, v_all = refs[9 + 4 * NEAR :]
    offset = SPAN - 1
    key_acc[...] = jnp.zeros_like(key_acc)
    value_acc[...] = jnp.zeros_like(value_acc)
    dq_ref[...] = jnp.zeros_like(dq_ref)
    join_pieces(
        first_ref, bound_ref, q_ref, g_ref, near_refs, piece_refs, m_ref, l_ref, d_in, k_all, v_all
    )
    lse_ref[...] = m_ref[...] * EXP2_SCALE + jnp.log2(l_ref[...])
    d_ref[...] = d_in[...] / l_ref[...]

    def begin(t):
        rows = tile_rows(t)
        one = pl.ds(t, 1)
        scores = dot(k_ref[...], q_ref[rows, :], 1, 1)
        scores = masked_scores(scores, bound_ref[one, :], offset, t)
        prob_grad = dot(v_ref[...], g_ref[rows, :], 1, 1)
        before = m_ref[one, :]
        top = jnp.maximum(jnp.max(scores, 0, keepdims=True), before)
        unscaled = jnp.exp2(scores * EXP2_SCALE - top * EXP2_SCALE)
        decay = jnp.exp2((before - top) * EXP2_SCALE)
        total = jnp.sum(unscaled, 0, keepdims=True) + l_ref[one, :] * decay
        product = jnp.sum(unscaled * prob_grad, 0, keepdims=True) + d_in[one, :] * decay
        inverse = 1.0 / total
        row_dot = product * inverse
        lse_ref[one, :] = top * EXP2_SCALE + jnp.log2(total)
        d_ref[one, :] = row_dot
        prob = unscaled * inverse
        score_grad = (prob * (prob_grad - row_dot)).astype(BF16)
        return prob.astype(BF16), score_grad

    def finish(t, prob, score_grad):
        rows = tile_rows(t)
        value_acc[...] += dot(prob, g_ref[rows, :], 1, 0)
        key_acc[...] += dot(score_grad, q_ref[rows, :], 1, 0)
        dq_ref[:, rows] = dot(k_ref[...], score_grad, 0, 0)

    over_tiles(first_ref, offset, begin, finish)
    pair_ref[0] = (key_acc[...] * SCALE).astype(pair_ref.dtype)
    pair_ref[1] = value_acc[...].astype(pair_ref.dtype)


def far_grad(first, bounds, q, g, kv, pieces):
    row = jax.ShapeDtypeStruct((TILES, ROWS), F32)
    operands = [first, bounds, q, g] + kv
    for piece in pieces:
        operands += list(piece)
    return pl.pallas_call(
        far_kernel,
        in_specs=[SMEM] + [VMEM] * (len(operands) - 1),
        out_specs=[VMEM] * 4,
        out_shape=[
            row,
            row,
            jax.ShapeDtypeStruct((WIDTH, TILES * ROWS), F32),
            jax.ShapeDtypeStruct((2, BLOCK, WIDTH), BF16),
        ],
        scratch_shapes=[pltpu.VMEM((BLOCK, WIDTH), F32)] * 2
        + [pltpu.VMEM((TILES, ROWS), F32)] * 3
        + [pltpu.VMEM((NEAR * BLOCK, WIDTH), BF16)] * 2,
        compiler_params=pltpu.CompilerParams(vmem_limit_bytes=40 << 20),
        cost_estimate=pl.CostEstimate(flops=8 << 30, bytes_accessed=1 << 10, transcendentals=0),
        name="grad_far",
    )(*operands)


def grad_kernel(offset, *refs):
    first_ref, bound_ref, q_ref, g_ref, kv_ref, m_ref, d_ref, dq_in = refs[:8]
    k_ref, v_ref = kv_ref.at[0], kv_ref.at[1]
    dq_ref, pair_ref, key_acc, value_acc = refs[8:]
    key_acc[...] = jnp.zeros_like(key_acc)
    value_acc[...] = jnp.zeros_like(value_acc)

    def begin(t):
        rows = tile_rows(t)
        one = pl.ds(t, 1)
        extent = own_extent(t) if offset == 0 else BLOCK
        scores = dot(k_ref[0:extent, :], q_ref[rows, :], 1, 1)
        scores = masked_scores(scores, bound_ref[one, :], offset, t)
        prob_grad = dot(v_ref[0:extent, :], g_ref[rows, :], 1, 1)
        prob = jnp.exp2(scores * EXP2_SCALE - m_ref[one, :])
        score_grad = (prob * (prob_grad - d_ref[one, :])).astype(BF16)
        return prob.astype(BF16), score_grad

    def finish(t, prob, score_grad):
        rows = tile_rows(t)
        extent = own_extent(t) if offset == 0 else BLOCK
        value_acc[0:extent, :] += dot(prob, g_ref[rows, :], 1, 0)
        key_acc[0:extent, :] += dot(score_grad, q_ref[rows, :], 1, 0)
        part = dot(k_ref[0:extent, :], score_grad, 0, 0)
        if offset == 0:
            dq_ref[rows, :] = jnp.transpose(((dq_in[:, rows] + part) * SCALE).astype(BF16))
        else:
            dq_ref[:, rows] += part

    over_tiles(first_ref, offset, begin, finish)
    pair_ref[0] = key_acc[...] * SCALE
    pair_ref[1] = value_acc[...]


def grad(offset, first, bounds, q, g, pair, lse, row_dot, dq):
    operands = [first, bounds, q, g, pair, lse, row_dot, dq]
    if offset:
        dq_shape = jax.ShapeDtypeStruct((WIDTH, TILES * ROWS), F32)
    else:
        dq_shape = jax.ShapeDtypeStruct((TILES * ROWS, WIDTH), BF16)
    return pl.pallas_call(
        functools.partial(grad_kernel, offset),
        in_specs=[SMEM] + [VMEM] * (len(operands) - 1),
        out_specs=[VMEM] * 2,
        out_shape=[dq_shape] + [jax.ShapeDtypeStruct((2, BLOCK, WIDTH), F32)],
        scratch_shapes=[pltpu.VMEM((BLOCK, WIDTH), F32)] * 2,
        input_output_aliases={7: 0} if offset else {},
        compiler_params=pltpu.CompilerParams(vmem_limit_bytes=40 << 20),
        cost_estimate=pl.CostEstimate(flops=(6 if offset else 5) << 30, bytes_accessed=1 << 10, transcendentals=0),
        name="grad_%d" % offset,
    )(*operands)


def ring(value, steps):
    count = lax.axis_size("ctx")
    return lax.ppermute(value, "ctx", [(s, (s + steps) % count) for s in range(count)])


def pair_swap(value):
    return lax.ppermute(value, "ctx", [(s, s ^ 1) for s in range(lax.axis_size("ctx"))])


def near_and_far(value):
    count = lax.axis_size("ctx")
    return lax.ppermute(
        value, "ctx", [(s, s + 1 if s % 2 == 0 else (s + 3) % count) for s in range(count)]
    )


def local(queries, key_heads, value_head_rows, out_grad, doc_start):
    block_len, head_count, head_width = queries.shape
    ctx = lax.axis_index("ctx")
    member = lax.axis_index("kv")
    members = lax.axis_size("kv")
    q = queries.reshape(block_len * head_count, head_width)
    g = out_grad.reshape(block_len * head_count, head_width)
    k = key_heads.reshape(block_len, head_width)
    v = value_head_rows.reshape(block_len, head_width)

    both = jnp.stack([k, v])
    both, doc_start = lax.optimization_barrier((both, doc_start))
    two = ring(both, 2)
    mixed = near_and_far(both)
    near = piece_stats(0, q, g, both)
    own = jnp.repeat(doc_start - ctx * block_len, head_count)[None, :]
    place = lax.broadcasted_iota(jnp.int32, (members, 1), 0)
    bounds = jnp.where(place == member, own, 0)
    step = 1
    while step < members:
        if step == 4:
            bounds, two = lax.optimization_barrier((bounds, two))
        bounds = bounds + lax.ppermute(bounds, "kv", [(s, s ^ step) for s in range(members)])
        step *= 2
    first = jnp.stack([bounds[:, 0], bounds[:, -1]], 1)

    even = ctx % 2 == 0
    swapped = pair_swap(two)
    one = jnp.where(even, swapped, mixed)
    three = jnp.where(even, mixed, swapped)
    kv = [both, one, two, three]
    pieces = [near] + [piece_stats(offset, q, g, kv[offset]) for offset in range(1, NEAR)]
    lse, row_dot, dq, chain = far_grad(first, bounds, q, g, kv, pieces)
    for offset in (2, 1):
        back = ring(chain, -1)
        dq, part = grad(offset, first, bounds, q, g, kv[offset], lse, row_dot, dq)
        chain = (part + back.astype(F32)).astype(BF16)
    back = ring(chain, -1)
    dq, part = grad(0, first, bounds, q, g, kv[0], lse, row_dot, dq)
    return (
        dq.reshape(queries.shape),
        (part[0] + back[0].astype(F32)).astype(BF16).reshape(key_heads.shape),
        (part[1] + back[1].astype(F32)).astype(BF16).reshape(value_head_rows.shape),
    )


def solution(mesh):
    return jax.shard_map(
        local,
        mesh=mesh,
        in_specs=(
            P("ctx", "kv", None),
            P("ctx", "kv", None),
            P("ctx", "kv", None),
            P("ctx", "kv", None),
            P(("ctx", "kv")),
        ),
        out_specs=(P("ctx", "kv", None), P("ctx", "kv", None), P("ctx", "kv", None)),
        check_vma=False,
    )
```
